256 devices in a mesh: seq: 32 (over x, y, core), vid: 8 (over z).
Axes of the slice: x: 4, y: 4, z: 8, core: 2. Of those that a mesh axis runs over, the one named last changes fastest.
Arguments:
- tokens: bfloat16 [262144, 768], P(('vid', 'seq')), parts along dimension 0, may hold values from -100 to 100
- latents: bfloat16 [4096, 768], P(('vid', 'seq')), parts along dimension 0, may hold values from -6 to 6
- read_weights: bfloat16 [4, 768, 768], P(None, 'seq'), may hold values from -1 to 1
- later_weights: bfloat16 [8, 768, 768], P(None, 'seq'), may hold values from -1 to 1
- head_scale: float32 [3, 12], replicated, may hold values from 1 to 40
Outputs:
- tokens_out: bfloat16 [262144, 768], P(('vid', 'seq')), parts along dimension 0
- latents_out: float32 [4096, 768], P(('vid', 'seq')), parts along dimension 0
The draws below stay inside these ranges and needn't reach their ends.
There are 8 independent parts, one for each index of `vid`. The reference program is written for one: setup_inputs(seed, part) draws one part's arguments, and reference() takes and returns one part's arrays. A program takes and returns all parts, laid end to end along the dimension named above; an argument that names none is the same for every part. Nothing has to cross between parts.
All inputs are finite; a program needn't handle non-finite values.
Results may differ from the reference program's by a relative error of at most 0.01.
The reference program's roundings to bfloat16 on the way count: a program that leaves them out, or rounds other values in their place, can miss the bound.
Values may be sent and summed in bfloat16 or wider, within the bound.
No kernel may reach another device: no remote copies, remote signals or barrier semaphores. Data moves between devices by JAX's collectives and lax.ppermute only.
A program may use at most 64 MiB of HBM per device.

```python
import math
import jax
import jax.numpy as jnp
from jax import lax

D = 768
HEADS = 12
LATENTS = 512
TOK_DEV = 1024
TOKENS = 32768


def latent_base(key):
    return jnp.clip(jax.random.normal(jax.random.fold_in(key, 11), (LATENTS, D), jnp.float32), -6.0, 6.0)


def draw_latents(key, part):
    return latent_base(key).astype(jnp.bfloat16)


def draw_tokens(key, part):
    slab_count = TOKENS // TOK_DEV
    slab_amp = jnp.exp(jax.random.uniform(jax.random.fold_in(key, 3), (slab_count, 1), jnp.float32, math.log(0.3), math.log(3.0)))
    centre = jax.random.normal(jax.random.fold_in(key, 4), (slab_count, D), jnp.float32) * slab_amp
    noise_rows = jax.random.normal(jax.random.fold_in(key, 5), (slab_count, TOK_DEV, D), jnp.float32)
    values = noise_rows + centre[:, None, :]
    return jnp.clip(values.reshape(TOKENS, D), -100.0, 100.0).astype(jnp.bfloat16)


def weight_stack(key, count):
    matrices = jax.random.normal(key, (count, D, D), jnp.float32) / math.sqrt(D)
    return jnp.clip(matrices, -6.0 / math.sqrt(D), 6.0 / math.sqrt(D))


def draw_read_weights(key, part):
    matrices = weight_stack(jax.random.fold_in(key, 21), 4)
    return matrices.astype(jnp.bfloat16)


def draw_later_weights(key, part):
    matrices = weight_stack(jax.random.fold_in(key, 22), 8)
    return matrices.astype(jnp.bfloat16)


def draw_head_scale(key, part):
    values = jnp.exp(jax.random.uniform(jax.random.fold_in(key, 31), (3, HEADS), jnp.float32, 0.0, math.log(4.0)))
    return values


def setup_inputs(seed: int = 0, part: int = 0) -> dict:
    seeds = jax.random.split(jax.random.key(seed), 6)
    own_keys = jax.random.split(jax.random.fold_in(seeds[5], part), 6)
    tokens = draw_tokens(jax.random.fold_in(jax.random.fold_in(seeds[5], part), 71), part)
    latents = draw_latents(jax.random.fold_in(jax.random.fold_in(seeds[5], part), 71), part)
    read_weights = draw_read_weights(jax.random.fold_in(seeds[5], 71), part)
    later_weights = draw_later_weights(jax.random.fold_in(seeds[5], 71), part)
    head_scale = draw_head_scale(jax.random.fold_in(seeds[5], 71), part)
    return {"tokens": tokens, "latents": latents, "read_weights": read_weights, "later_weights": later_weights, "head_scale": head_scale}


epsilon = 1e-06

def norm_rows(values):
    values = values.astype(jnp.float32)
    return values * lax.rsqrt(lax.optimization_barrier(jnp.mean(values * values, axis=-1, keepdims=True)) + epsilon)

def head_norm(values, n_heads):
    by_head = values.reshape(values.shape[0], n_heads, values.shape[1] // n_heads)
    by_head = by_head * lax.rsqrt(lax.optimization_barrier(jnp.mean(by_head * by_head, axis=-1, keepdims=True)) + epsilon)
    return by_head.reshape(values.shape).astype(jnp.bfloat16)

def project(inputs, weight):
    return jnp.dot(inputs, weight, preferred_element_type=jnp.float32)

def head_cols(values, head_index, head_dim):
    return lax.dynamic_slice_in_dim(values, head_index * head_dim, head_dim, 1)

def inner(left, right):
    return lax.dot_general(left, right, (((1,), (1,)), ((), ())), preferred_element_type=jnp.float32)

def attend(queries, key_rows, val_rows, factors, n_heads):
    head_dim = queries.shape[1] // n_heads

    def one_head(packed):
        head_index, factor = packed
        scores = inner(head_cols(queries, head_index, head_dim), head_cols(key_rows, head_index, head_dim)) * (factor / math.sqrt(head_dim))
        row_top = lax.optimization_barrier(jnp.max(scores, axis=1, keepdims=True))
        exp_scores = jnp.exp(scores - row_top)
        weights = (exp_scores / lax.optimization_barrier(jnp.sum(exp_scores, axis=1, keepdims=True))).astype(jnp.bfloat16)
        return jnp.dot(weights, head_cols(val_rows, head_index, head_dim), preferred_element_type=jnp.float32)
    results = lax.map(one_head, (jnp.arange(n_heads, dtype=jnp.int32), factors))
    return results.transpose(1, 0, 2).reshape(queries.shape).astype(jnp.bfloat16)

def read_parts(queries, key_rows, val_rows, factors, n_heads):
    head_dim = queries.shape[1] // n_heads

    def one_head(packed):
        head_index, factor = packed
        scores = inner(head_cols(queries, head_index, head_dim), head_cols(key_rows, head_index, head_dim)) * (factor / math.sqrt(head_dim))
        row_top = lax.optimization_barrier(jnp.max(scores, axis=1))
        exp_scores = jnp.exp(scores - row_top[:, None])
        totals = lax.optimization_barrier(jnp.sum(exp_scores, axis=1))
        summed = jnp.dot(exp_scores.astype(jnp.bfloat16), head_cols(val_rows, head_index, head_dim), preferred_element_type=jnp.float32)
        return (summed.astype(jnp.bfloat16), row_top, totals)
    return lax.map(one_head, (jnp.arange(n_heads, dtype=jnp.int32), factors))

def reference(tokens, latents, read_weights, later_weights, head_scale):
    tok_normed = norm_rows(tokens).astype(jnp.bfloat16)
    read_q = head_norm(project(norm_rows(latents).astype(jnp.bfloat16), read_weights[0]), HEADS)
    read_k = head_norm(project(tok_normed, read_weights[1]), HEADS)
    read_v = project(tok_normed, read_weights[2]).astype(jnp.bfloat16)
    slab_count = TOKENS // TOK_DEV
    key_slabs = read_k.reshape(slab_count, TOK_DEV, D)
    val_slabs = read_v.reshape(slab_count, TOK_DEV, D)

    def one_slab(slab_pair):
        return read_parts(read_q, slab_pair[0], slab_pair[1], head_scale[0], HEADS)
    partials, row_tops, totals = lax.map(one_slab, (key_slabs, val_slabs))
    row_best = lax.optimization_barrier(jnp.max(row_tops, axis=0))
    rescale = jnp.exp(row_tops - row_best[None])
    summed = lax.optimization_barrier(jnp.sum(partials.astype(jnp.float32) * rescale[..., None], axis=0))
    weight_sum = lax.optimization_barrier(jnp.sum(totals * rescale, axis=0))
    read_mixed = summed / weight_sum[..., None]
    read_mix = read_mixed.transpose(1, 0, 2).reshape(LATENTS, D).astype(jnp.bfloat16)
    lat_one = latents.astype(jnp.float32) + project(read_mix, read_weights[3])
    self_normed = norm_rows(lat_one).astype(jnp.bfloat16)
    self_q = head_norm(project(self_normed, later_weights[0]), HEADS)
    self_k = head_norm(project(self_normed, later_weights[1]), HEADS)
    self_v = project(self_normed, later_weights[2]).astype(jnp.bfloat16)
    latents_out = lat_one + project(attend(self_q, self_k, self_v, head_scale[1], HEADS), later_weights[3])
    write_in = norm_rows(latents_out).astype(jnp.bfloat16)
    write_q = head_norm(project(tok_normed, later_weights[4]), HEADS)
    write_k = head_norm(project(write_in, later_weights[5]), HEADS)
    write_v = project(write_in, later_weights[6]).astype(jnp.bfloat16)
    tokens_out = (tokens.astype(jnp.float32) + project(attend(write_q, write_k, write_v, head_scale[2], HEADS), later_weights[7])).astype(jnp.bfloat16)
    return (tokens_out, latents_out)
```

```python
import functools
import math

import jax
import jax.numpy as jnp
from jax import lax
from jax.experimental import pallas as pl
from jax.experimental.pallas import tpu as pltpu
from jax.sharding import PartitionSpec as P

HEADS = 12
HEAD_DIM = 64
PAIR = 2 * HEAD_DIM
EPSILON = 1e-06
LOG2E = math.log2(math.e)
BF16 = jnp.bfloat16
F32 = jnp.float32
VMEM_LIMIT = 56 * 1024 * 1024
PIECE = 20
ODD_TOTALS = 12
EVEN_TOTALS = 64


def norm_rows(values):
    values = values.astype(F32)
    return values * lax.rsqrt(jnp.mean(values * values, axis=-1, keepdims=True) + EPSILON)


def dot(left, right):
    return jnp.dot(left, right, preferred_element_type=F32)


def dot_nt(left, right):
    return lax.dot_general(left, right, (((1,), (1,)), ((), ())), preferred_element_type=F32)


def head_mean_matrix():
    rows = lax.broadcasted_iota(jnp.int32, (256, 256), 0) // HEAD_DIM
    cols = lax.broadcasted_iota(jnp.int32, (256, 256), 1) // HEAD_DIM
    return jnp.where(rows == cols, 1.0 / HEAD_DIM, 0.0).astype(BF16)


def head_norm(values, mean_matrix):
    squares = values * values
    high = squares.astype(BF16)
    low = (squares - high.astype(F32)).astype(BF16)
    parts = []
    for start in range(0, values.shape[1], 256):
        cols = slice(start, start + 256)
        mean = dot(high[:, cols], mean_matrix) + dot(low[:, cols], mean_matrix)
        parts.append((values[:, cols] * lax.rsqrt(mean + EPSILON)).astype(BF16))
    return jnp.concatenate(parts, axis=1)


def first_half(shape):
    return lax.broadcasted_iota(jnp.int32, shape, 1) % PAIR < HEAD_DIM


def row_blocks(n_rows, block, body):
    def step(i, carry):
        body(pl.ds(pl.multiple_of(i * block, block), block))
        return carry

    lax.fori_loop(0, n_rows // block, step, 0)


def project_heads(x_ref, weight, mean_matrix, out_ref, block=256):
    def body(rows):
        out_ref[rows, :] = head_norm(dot(x_ref[rows, :], weight[...]), mean_matrix)

    row_blocks(x_ref.shape[0], block, body)


def project_values(x_ref, weight, even_ref, odd_ref, block=256):
    def body(rows):
        values = dot(x_ref[rows, :], weight[...]).astype(BF16)
        mask = first_half(values.shape)
        one = jnp.ones_like(values)
        even_ref[rows, :] = jnp.where(mask, values, one)
        odd_ref[rows, :] = jnp.where(mask, one, values)

    row_blocks(x_ref.shape[0], block, body)


def pair_parts(queries, keys, even, odd, even_factor, odd_factor):
    mask = first_half(queries.shape)
    zero = jnp.zeros_like(queries)
    scores_even = dot_nt(jnp.where(mask, queries, zero), keys)
    scores_odd = dot_nt(jnp.where(mask, zero, queries), keys)
    top_even = jnp.max(scores_even, axis=1, keepdims=True)
    exp_even = jnp.exp2((scores_even - top_even) * (even_factor * LOG2E)).astype(BF16)
    top_odd = jnp.max(scores_odd, axis=1, keepdims=True)
    exp_odd = jnp.exp2((scores_odd - top_odd) * (odd_factor * LOG2E)).astype(BF16)
    return top_even, top_odd, dot(exp_even, even), dot(exp_odd, odd)


def factors(scale_ref, stage, pair):
    root = math.sqrt(HEAD_DIM)
    return scale_ref[stage, 2 * pair] / root, scale_ref[stage, 2 * pair + 1] / root


def attend(q_ref, k_ref, even_ref, odd_ref, scale_ref, stage, out_ref, block=256):
    n_blocks = q_ref.shape[0] // block

    def step(i, carry):
        pair, row = i // n_blocks, i % n_blocks
        cols = pl.ds(pl.multiple_of(pair * PAIR, PAIR), PAIR)
        rows = pl.ds(pl.multiple_of(row * block, block), block)
        _, _, even, odd = pair_parts(
            q_ref[rows, cols],
            k_ref[:, cols],
            even_ref[:, cols],
            odd_ref[:, cols],
            *factors(scale_ref, stage, pair),
        )
        mask = first_half(even.shape)
        summed = jnp.where(mask, even, odd)
        total = pltpu.roll(jnp.where(mask, odd, even), HEAD_DIM, 1)
        out_ref[rows, cols] = (summed / total).astype(BF16)
        return carry

    lax.fori_loop(0, n_blocks * (HEADS // 2), step, 0)


def read_kernel(
    tok_ref, lat_ref, weight_ref, scale_ref, out_ref, q_ref, k_ref, even_ref, odd_ref, extra_ref
):
    mean_matrix = head_mean_matrix()
    width = tok_ref.shape[1]
    project_heads(lat_ref, weight_ref.at[0], mean_matrix, q_ref)
    project_heads(tok_ref, weight_ref.at[1], mean_matrix, k_ref)
    project_values(tok_ref, weight_ref.at[2], even_ref, odd_ref)
    extra_ref[...] = jnp.zeros_like(extra_ref)
    block = 256
    n_blocks = lat_ref.shape[0] // block

    def step(i, carry):
        pair, row = i // n_blocks, i % n_blocks
        cols = pl.ds(pl.multiple_of(pair * PAIR, PAIR), PAIR)
        rows = pl.ds(pl.multiple_of(row * block, block), block)
        even_factor, odd_factor = factors(scale_ref, 0, pair)
        top_even, top_odd, even, odd = pair_parts(
            q_ref[rows, cols],
            k_ref[:, cols],
            even_ref[:, cols],
            odd_ref[:, cols],
            even_factor,
            odd_factor,
        )
        out_ref[rows, cols] = jnp.where(first_half(even.shape), even, odd).astype(BF16)
        lane = lax.broadcasted_iota(jnp.int32, even.shape, 1)
        extra = extra_ref[rows, :]
        extra = jnp.where(lane == 2 * pair, top_even * even_factor, extra)
        extra = jnp.where(lane == 2 * pair + 1, top_odd * odd_factor, extra)
        extra = jnp.where(lane == EVEN_TOTALS + pair, even, extra)
        extra = jnp.where(lane == ODD_TOTALS + pair, odd, extra)
        extra_ref[rows, :] = extra
        return carry

    lax.fori_loop(0, n_blocks * (HEADS // 2), step, 0)
    extra = extra_ref[...]
    high = extra.astype(BF16).astype(F32)
    mid = (extra - high).astype(BF16).astype(F32)
    low = extra - high - mid
    packed = high + pltpu.roll(mid, PIECE, 1) + pltpu.roll(low, 2 * PIECE, 1)
    out_ref[:, width:] = packed.astype(BF16)


def combine_kernel(part_ref, out_ref, *, slabs):
    width = out_ref.shape[-1]
    own_rows = out_ref.shape[1]
    lane = lax.broadcasted_iota(jnp.int32, (PAIR, width), 0)
    head = lax.broadcasted_iota(jnp.int32, (PAIR, width), 1) // HEAD_DIM
    total_lane = jnp.where(head % 2 == 0, EVEN_TOTALS, ODD_TOTALS) + head // 2
    pick_top = jnp.zeros((PAIR, width), F32)
    pick_total = jnp.zeros((PAIR, width), F32)
    for piece in range(3):
        pick_top = jnp.where(lane == head + piece * PIECE, 1.0, pick_top)
        pick_total = jnp.where(lane == total_lane + piece * PIECE, 1.0, pick_total)
    extra = part_ref[:, width:]
    shape = (slabs, own_rows, width)
    tops = dot(extra, pick_top.astype(BF16)).reshape(shape)
    totals = dot(extra, pick_total.astype(BF16)).reshape(shape)
    rescale = jnp.exp(tops - jnp.max(tops, axis=0, keepdims=True))
    sums = part_ref[:, :width].astype(F32).reshape(shape)
    mixed = jnp.sum(rescale * sums, axis=0) / jnp.sum(rescale * totals, axis=0)
    out_ref[...] = jnp.broadcast_to(mixed.astype(BF16)[None], out_ref.shape)


def write_kernel(
    index_ref,
    scale_ref,
    mix_ref,
    lat_ref,
    out_weight_ref,
    weight_ref,
    raw_ref,
    tok_ref,
    tok_out_ref,
    lat_out_ref,
    stream_ref,
    normed_ref,
    q_ref,
    k_ref,
    even_ref,
    odd_ref,
    att_ref,
    write_q_ref,
    write_att_ref,
):
    mean_matrix = head_mean_matrix()
    n_lat = lat_ref.shape[0]
    own_rows = lat_out_ref.shape[0]

    def first(rows):
        lat_one = lat_ref[rows, :].astype(F32) + dot(mix_ref[rows, :], out_weight_ref[...])
        stream_ref[rows, :] = lat_one
        normed_ref[rows, :] = norm_rows(lat_one).astype(BF16)

    row_blocks(n_lat, 256, first)
    project_heads(normed_ref, weight_ref.at[0], mean_matrix, q_ref)
    project_heads(normed_ref, weight_ref.at[1], mean_matrix, k_ref)
    project_values(normed_ref, weight_ref.at[2], even_ref, odd_ref)
    attend(q_ref, k_ref, even_ref, odd_ref, scale_ref, 1, att_ref)

    def second(rows):
        lat_two = stream_ref[rows, :] + dot(att_ref[rows, :], weight_ref[3])
        stream_ref[rows, :] = lat_two
        normed_ref[rows, :] = norm_rows(lat_two).astype(BF16)

    row_blocks(n_lat, 256, second)
    own = pl.ds(pl.multiple_of(index_ref[0] * own_rows, own_rows), own_rows)
    lat_out_ref[...] = stream_ref[own, :]
    project_heads(normed_ref, weight_ref.at[5], mean_matrix, k_ref)
    project_values(normed_ref, weight_ref.at[6], even_ref, odd_ref)
    project_heads(tok_ref, weight_ref.at[4], mean_matrix, write_q_ref)
    attend(write_q_ref, k_ref, even_ref, odd_ref, scale_ref, 2, write_att_ref)

    def last(rows):
        update = dot(write_att_ref[rows, :], weight_ref[7])
        tok_out_ref[rows, :] = (raw_ref[rows, :].astype(F32) + update).astype(BF16)

    row_blocks(raw_ref.shape[0], 256, last)


IN_VMEM = pl.BlockSpec(memory_space=pltpu.VMEM)
IN_SMEM = pl.BlockSpec(memory_space=pltpu.SMEM)


def shards(tokens, latents, read_weights, later_weights, head_scale):
    n_tok, width = tokens.shape
    own_rows = latents.shape[0]
    slabs = lax.axis_size("seq")
    n_lat = own_rows * slabs
    read_full = lax.all_gather(read_weights, "seq", axis=1, tiled=True)
    later_full = lax.all_gather(later_weights, "seq", axis=1, tiled=True)
    lat_full = lax.all_gather(latents, "seq", axis=0, tiled=True)
    tok_normed = norm_rows(tokens).astype(BF16)
    lat_normed = norm_rows(lat_full).astype(BF16)
    params = pltpu.CompilerParams(vmem_limit_bytes=VMEM_LIMIT)
    parts = pl.pallas_call(
        read_kernel,
        name="read",
        out_shape=jax.ShapeDtypeStruct((n_lat, width + PAIR), BF16),
        in_specs=[IN_VMEM, IN_VMEM, IN_VMEM, IN_SMEM],
        out_specs=IN_VMEM,
        scratch_shapes=[
            pltpu.VMEM((n_lat, width), BF16),
            pltpu.VMEM((n_tok, width), BF16),
            pltpu.VMEM((n_tok, width), BF16),
            pltpu.VMEM((n_tok, width), BF16),
            pltpu.VMEM((n_lat, PAIR), F32),
        ],
        compiler_params=params,
        cost_estimate=pl.CostEstimate(
            flops=20_000_000_000, bytes_accessed=8_000_000, transcendentals=6_300_000
        ),
    )(tok_normed, lat_normed, read_full[:3], head_scale)
    parts = lax.all_to_all(parts, "seq", 0, 0, tiled=True)
    mixed = pl.pallas_call(
        functools.partial(combine_kernel, slabs=slabs),
        name="combine",
        out_shape=jax.ShapeDtypeStruct((slabs, own_rows, width), BF16),
        in_specs=[IN_VMEM],
        out_specs=IN_VMEM,
        compiler_params=params,
    )(parts)
    mixed = lax.all_to_all(mixed, "seq", 0, 0, tiled=True).reshape(n_lat, width)
    index = lax.axis_index("seq").astype(jnp.int32).reshape(1)
    return pl.pallas_call(
        write_kernel,
        name="write",
        out_shape=(
            jax.ShapeDtypeStruct(tokens.shape, BF16),
            jax.ShapeDtypeStruct(latents.shape, F32),
        ),
        in_specs=[IN_SMEM, IN_SMEM] + [IN_VMEM] * 6,
        out_specs=(IN_VMEM, IN_VMEM),
        scratch_shapes=[
            pltpu.VMEM((n_lat, width), F32),
            pltpu.VMEM((n_lat, width), BF16),
            pltpu.VMEM((n_lat, width), BF16),
            pltpu.VMEM((n_lat, width), BF16),
            pltpu.VMEM((n_lat, width), BF16),
            pltpu.VMEM((n_lat, width), BF16),
            pltpu.VMEM((n_lat, width), BF16),
            pltpu.VMEM((n_tok, width), BF16),
            pltpu.VMEM((n_tok, width), BF16),
        ],
        compiler_params=params,
    )(index, head_scale, mixed, lat_full, read_full[3], later_full, tokens, tok_normed)


def solution(mesh):
    placed = (
        P(("vid", "seq"), None),
        P(("vid", "seq"), None),
        P(None, "seq", None),
        P(None, "seq", None),
        P(),
    )
    return jax.shard_map(
        shards,
        mesh=mesh,
        in_specs=placed,
        out_specs=(P(("vid", "seq"), None), P(("vid", "seq"), None)),
        check_vma=False,
    )
```

```python
import functools
import math

import jax
import jax.numpy as jnp
from jax import lax
from jax.experimental import pallas as pl
from jax.experimental.pallas import tpu as pltpu
from jax.sharding import PartitionSpec as P

HEADS = 12
HEAD_DIM = 64
PAIR = 2 * HEAD_DIM
EPSILON = 1e-06
LOG2E = math.log2(math.e)
BF16 = jnp.bfloat16
F32 = jnp.float32
VMEM_LIMIT = 56 * 1024 * 1024
PIECE = 20
ODD_TOTALS = 12
EVEN_TOTALS = 64
CORES = 2


def norm_rows(values):
    values = values.astype(F32)
    return values * lax.rsqrt(jnp.mean(values * values, axis=-1, keepdims=True) + EPSILON)


def dot(left, right):
    return jnp.dot(left, right, preferred_element_type=F32)


def dot_nt(left, right):
    return lax.dot_general(left, right, (((1,), (1,)), ((), ())), preferred_element_type=F32)


def head_mean_matrix():
    rows = lax.broadcasted_iota(jnp.int32, (256, 256), 0) // HEAD_DIM
    cols = lax.broadcasted_iota(jnp.int32, (256, 256), 1) // HEAD_DIM
    return jnp.where(rows == cols, 1.0 / HEAD_DIM, 0.0).astype(BF16)


def head_norm(values, mean_matrix):
    squares = values * values
    high = squares.astype(BF16)
    low = (squares - high.astype(F32)).astype(BF16)
    parts = []
    for start in range(0, values.shape[1], 256):
        cols = slice(start, min(start + 256, values.shape[1]))
        size = cols.stop - start
        matrix = mean_matrix[:size, :size]
        mean = dot(high[:, cols], matrix) + dot(low[:, cols], matrix)
        parts.append((values[:, cols] * lax.rsqrt(mean + EPSILON)).astype(BF16))
    return jnp.concatenate(parts, axis=1)


def first_half(shape):
    return lax.broadcasted_iota(jnp.int32, shape, 1) % PAIR < HEAD_DIM


def row_blocks(n_rows, block, body):
    def step(i, carry):
        body(pl.ds(pl.multiple_of(i * block, block), block))
        return carry

    lax.fori_loop(0, n_rows // block, step, 0)


def project_heads(x_ref, weight, mean_matrix, out_ref, block=256):
    def body(rows):
        out_ref[rows, :] = head_norm(dot(x_ref[rows, :], weight[...]), mean_matrix)

    row_blocks(x_ref.shape[0], block, body)


def project_values(x_ref, weight, even_ref, odd_ref, block=256):
    def body(rows):
        values = dot(x_ref[rows, :], weight[...]).astype(BF16)
        mask = first_half(values.shape)
        one = jnp.ones_like(values)
        even_ref[rows, :] = jnp.where(mask, values, one)
        odd_ref[rows, :] = jnp.where(mask, one, values)

    row_blocks(x_ref.shape[0], block, body)


def pair_parts(queries, keys, even, odd, even_factor, odd_factor):
    mask = first_half(queries.shape)
    zero = jnp.zeros_like(queries)
    scores_even = dot_nt(jnp.where(mask, queries, zero), keys)
    scores_odd = dot_nt(jnp.where(mask, zero, queries), keys)
    top_even = jnp.max(scores_even, axis=1, keepdims=True)
    exp_even = jnp.exp2((scores_even - top_even) * (even_factor * LOG2E)).astype(BF16)
    top_odd = jnp.max(scores_odd, axis=1, keepdims=True)
    exp_odd = jnp.exp2((scores_odd - top_odd) * (odd_factor * LOG2E)).astype(BF16)
    return top_even, top_odd, dot(exp_even, even), dot(exp_odd, odd)


def factors(scale_ref, stage, head):
    root = math.sqrt(HEAD_DIM)
    return scale_ref[stage, head] / root, scale_ref[stage, head + 1] / root


def attend(q_ref, k_ref, even_ref, odd_ref, scale_ref, stage, out_ref, block=256):
    n_blocks = q_ref.shape[0] // block

    def step(i, carry):
        pair, row = i // n_blocks, i % n_blocks
        cols = pl.ds(pl.multiple_of(pair * PAIR, PAIR), PAIR)
        rows = pl.ds(pl.multiple_of(row * block, block), block)
        _, _, even, odd = pair_parts(
            q_ref[rows, cols],
            k_ref[:, cols],
            even_ref[:, cols],
            odd_ref[:, cols],
            *factors(scale_ref, stage, 2 * pair),
        )
        mask = first_half(even.shape)
        summed = jnp.where(mask, even, odd)
        total = pltpu.roll(jnp.where(mask, odd, even), HEAD_DIM, 1)
        out_ref[rows, cols] = (summed / total).astype(BF16)
        return carry

    lax.fori_loop(0, n_blocks * (HEADS // 2), step, 0)


def read_kernel(
    core_ref,
    scale_ref,
    own_ref,
    peer_ref,
    lat_ref,
    weight_ref,
    out_ref,
    q_ref,
    k_ref,
    even_ref,
    odd_ref,
    extra_ref,
):
    mean_matrix = head_mean_matrix()
    width = q_ref.shape[1]
    heads = width // HEAD_DIM
    n_tok = own_ref.shape[0]
    columns = [pl.ds(i * width, width) for i in range(3)]
    project_heads(lat_ref, weight_ref.at[:, columns[0]], mean_matrix, q_ref)
    for slab, tok_ref in enumerate((own_ref, peer_ref)):
        rows = pl.ds(slab * n_tok, n_tok)
        project_heads(tok_ref, weight_ref.at[:, columns[1]], mean_matrix, k_ref.at[rows, :])
        project_values(
            tok_ref, weight_ref.at[:, columns[2]], even_ref.at[rows, :], odd_ref.at[rows, :]
        )
    extra_ref[...] = jnp.zeros_like(extra_ref)
    block = 256
    n_blocks = lat_ref.shape[0] // block

    def step(i, carry):
        pair, row = i // n_blocks, i % n_blocks
        cols = pl.ds(pl.multiple_of(pair * PAIR, PAIR), PAIR)
        rows = pl.ds(pl.multiple_of(row * block, block), block)
        even_factor, odd_factor = factors(scale_ref, 0, core_ref[0] * heads + 2 * pair)
        top_even, top_odd, even, odd = pair_parts(
            q_ref[rows, cols],
            k_ref[:, cols],
            even_ref[:, cols],
            odd_ref[:, cols],
            even_factor,
            odd_factor,
        )
        out_ref[rows, cols] = jnp.where(first_half(even.shape), even, odd).astype(BF16)
        lane = lax.broadcasted_iota(jnp.int32, even.shape, 1)
        extra = extra_ref[rows, :]
        extra = jnp.where(lane == 2 * pair, top_even * even_factor, extra)
        extra = jnp.where(lane == 2 * pair + 1, top_odd * odd_factor, extra)
        extra = jnp.where(lane == EVEN_TOTALS + pair, even, extra)
        extra = jnp.where(lane == ODD_TOTALS + pair, odd, extra)
        extra_ref[rows, :] = extra
        return carry

    lax.fori_loop(0, n_blocks * (heads // 2), step, 0)
    extra = extra_ref[...]
    high = extra.astype(BF16).astype(F32)
    mid = (extra - high).astype(BF16).astype(F32)
    low = extra - high - mid
    packed = high + pltpu.roll(mid, PIECE, 1) + pltpu.roll(low, 2 * PIECE, 1)
    out_ref[:, width:] = packed.astype(BF16)


def combine_kernel(part_ref, out_ref, *, parts):
    width = out_ref.shape[-1]
    rows = out_ref.shape[1]
    lane = lax.broadcasted_iota(jnp.int32, (PAIR, width), 0)
    head = lax.broadcasted_iota(jnp.int32, (PAIR, width), 1) // HEAD_DIM
    total_lane = jnp.where(head % 2 == 0, EVEN_TOTALS, ODD_TOTALS) + head // 2
    pick_top = jnp.zeros((PAIR, width), F32)
    pick_total = jnp.zeros((PAIR, width), F32)
    for piece in range(3):
        pick_top = jnp.where(lane == head + piece * PIECE, 1.0, pick_top)
        pick_total = jnp.where(lane == total_lane + piece * PIECE, 1.0, pick_total)
    extra = part_ref[:, width:]
    shape = (parts, rows, width)
    tops = dot(extra, pick_top.astype(BF16)).reshape(shape)
    totals = dot(extra, pick_total.astype(BF16)).reshape(shape)
    rescale = jnp.exp(tops - jnp.max(tops, axis=0, keepdims=True))
    sums = part_ref[:, :width].astype(F32).reshape(shape)
    mixed = jnp.sum(rescale * sums, axis=0) / jnp.sum(rescale * totals, axis=0)
    out_ref[...] = jnp.broadcast_to(mixed.astype(BF16)[None], out_ref.shape)


def write_kernel(
    index_ref,
    scale_ref,
    mix_ref,
    lat_ref,
    weight_ref,
    raw_ref,
    tok_ref,
    tok_out_ref,
    lat_out_ref,
    stream_ref,
    normed_ref,
    q_ref,
    k_ref,
    even_ref,
    odd_ref,
    att_ref,
    write_q_ref,
    write_att_ref,
):
    mean_matrix = head_mean_matrix()
    n_lat = lat_ref.shape[0]
    own_rows = lat_out_ref.shape[0]

    chips, cores, chip_rows, half = mix_ref.shape
    step = 256 // chip_rows

    def first(chip, carry):
        rows = pl.ds(pl.multiple_of(chip * 256, 256), 256)
        lat_one = lat_ref[rows, :].astype(F32)
        for core in range(cores):
            mix = mix_ref[pl.ds(chip * step, step), core].reshape(256, half)
            lat_one += dot(mix, weight_ref[0, core * half : (core + 1) * half, :])
        stream_ref[rows, :] = lat_one
        normed_ref[rows, :] = norm_rows(lat_one).astype(BF16)
        return carry

    lax.fori_loop(0, n_lat // 256, first, 0)
    project_heads(normed_ref, weight_ref.at[1], mean_matrix, q_ref)
    project_heads(normed_ref, weight_ref.at[2], mean_matrix, k_ref)
    project_values(normed_ref, weight_ref.at[3], even_ref, odd_ref)
    attend(q_ref, k_ref, even_ref, odd_ref, scale_ref, 1, att_ref)

    def second(rows):
        lat_two = stream_ref[rows, :] + dot(att_ref[rows, :], weight_ref[4])
        stream_ref[rows, :] = lat_two
        normed_ref[rows, :] = norm_rows(lat_two).astype(BF16)

    row_blocks(n_lat, 256, second)
    own = pl.ds(pl.multiple_of(index_ref[0] * own_rows, own_rows), own_rows)
    lat_out_ref[...] = stream_ref[own, :]
    project_heads(normed_ref, weight_ref.at[6], mean_matrix, k_ref)
    project_values(normed_ref, weight_ref.at[7], even_ref, odd_ref)
    project_heads(tok_ref, weight_ref.at[5], mean_matrix, write_q_ref)
    attend(write_q_ref, k_ref, even_ref, odd_ref, scale_ref, 2, write_att_ref)

    def last(rows):
        update = dot(write_att_ref[rows, :], weight_ref[8])
        tok_out_ref[rows, :] = (raw_ref[rows, :].astype(F32) + update).astype(BF16)

    row_blocks(raw_ref.shape[0], 256, last)


IN_VMEM = pl.BlockSpec(memory_space=pltpu.VMEM)
IN_SMEM = pl.BlockSpec(memory_space=pltpu.SMEM)


def shards(tokens, latents, read_weights, later_weights, head_scale):
    n_tok, width = tokens.shape
    own_rows = latents.shape[0]
    devices = lax.axis_size("seq")
    chips = devices // CORES
    n_lat = own_rows * devices
    half = width // CORES
    weight_rows = read_weights.shape[1]
    index = lax.axis_index("seq").astype(jnp.int32)
    same_core = [[CORES * chip + core for chip in range(chips)] for core in range(CORES)]
    swap = [(device, device ^ 1) for device in range(devices)]

    first = read_weights[:3].reshape(3, weight_rows, CORES, half).transpose(2, 1, 0, 3)
    first = first.reshape(1, CORES, weight_rows, 3 * half)
    first = jnp.broadcast_to(first, (chips,) + first.shape[1:])
    first = first.reshape(devices, weight_rows, 3 * half)
    first = lax.all_to_all(first, "seq", 0, 0, tiled=True).reshape(width, 3 * half)
    rest = jnp.concatenate([read_weights[3:], later_weights])
    rest = lax.all_gather(rest, "seq", axis=1, tiled=True)
    lat_full = lax.all_gather(latents, "seq", axis=0, tiled=True)
    tok_normed = norm_rows(tokens).astype(BF16)
    peer_normed = lax.ppermute(tok_normed, "seq", swap)
    lat_normed = norm_rows(lat_full).astype(BF16)
    params = pltpu.CompilerParams(vmem_limit_bytes=VMEM_LIMIT)
    parts = pl.pallas_call(
        read_kernel,
        name="read",
        out_shape=jax.ShapeDtypeStruct((n_lat, half + PAIR), BF16),
        in_specs=[IN_SMEM, IN_SMEM] + [IN_VMEM] * 4,
        out_specs=IN_VMEM,
        scratch_shapes=[
            pltpu.VMEM((n_lat, half), BF16),
            pltpu.VMEM((2 * n_tok, half), BF16),
            pltpu.VMEM((2 * n_tok, half), BF16),
            pltpu.VMEM((2 * n_tok, half), BF16),
            pltpu.VMEM((n_lat, PAIR), F32),
        ],
        compiler_params=params,
        cost_estimate=pl.CostEstimate(
            flops=20_000_000_000, bytes_accessed=8_000_000, transcendentals=6_300_000
        ),
    )((index % CORES).reshape(1), head_scale, tok_normed, peer_normed, lat_normed, first)
    parts = lax.all_to_all(
        parts.reshape(chips, CORES * own_rows, half + PAIR),
        "seq",
        0,
        0,
        tiled=True,
        axis_index_groups=same_core,
    )
    mixed = pl.pallas_call(
        functools.partial(combine_kernel, parts=chips),
        name="combine",
        out_shape=jax.ShapeDtypeStruct((devices, CORES * own_rows, half), BF16),
        in_specs=[IN_VMEM],
        out_specs=IN_VMEM,
        compiler_params=params,
    )(parts.reshape(n_lat, half + PAIR))
    mixed = lax.all_to_all(mixed, "seq", 0, 0, tiled=True)
    mixed = mixed.reshape(chips, CORES, CORES * own_rows, half)
    return pl.pallas_call(
        write_kernel,
        name="write",
        out_shape=(
            jax.ShapeDtypeStruct(tokens.shape, BF16),
            jax.ShapeDtypeStruct(latents.shape, F32),
        ),
        in_specs=[IN_SMEM, IN_SMEM] + [IN_VMEM] * 5,
        out_specs=(IN_VMEM, IN_VMEM),
        scratch_shapes=[
            pltpu.VMEM((n_lat, width), F32),
            pltpu.VMEM((n_lat, width), BF16),
            pltpu.VMEM((n_lat, width), BF16),
            pltpu.VMEM((n_lat, width), BF16),
            pltpu.VMEM((n_lat, width), BF16),
            pltpu.VMEM((n_lat, width), BF16),
            pltpu.VMEM((n_lat, width), BF16),
            pltpu.VMEM((n_tok, width), BF16),
            pltpu.VMEM((n_tok, width), BF16),
        ],
        compiler_params=params,
    )(index.reshape(1), head_scale, mixed, lat_full, rest, tokens, tok_normed)


def solution(mesh):
    placed = (
        P(("vid", "seq"), None),
        P(("vid", "seq"), None),
        P(None, "seq", None),
        P(None, "seq", None),
        P(),
    )
    return jax.shard_map(
        shards,
        mesh=mesh,
        in_specs=placed,
        out_specs=(P(("vid", "seq"), None), P(("vid", "seq"), None)),
        check_vma=False,
    )
```

```python
import functools
import math

import jax
import jax.numpy as jnp
from jax import lax
from jax.experimental import pallas as pl
from jax.experimental.pallas import tpu as pltpu
from jax.sharding import PartitionSpec as P

HEADS = 12
HEAD_DIM = 64
PAIR = 2 * HEAD_DIM
EPSILON = 1e-06
LOG2E = math.log2(math.e)
BF16 = jnp.bfloat16
F32 = jnp.float32
VMEM_LIMIT = 56 * 1024 * 1024
PIECE = 16
TOTALS = 6
CORES = 2


def norm_rows(values):
    values = values.astype(F32)
    return values * lax.rsqrt(jnp.mean(values * values, axis=-1, keepdims=True) + EPSILON)


def dot(left, right):
    return jnp.dot(left, right, preferred_element_type=F32)


def dot_nt(left, right):
    return lax.dot_general(left, right, (((1,), (1,)), ((), ())), preferred_element_type=F32)


def head_mean_matrix():
    rows = lax.broadcasted_iota(jnp.int32, (256, 256), 0) // HEAD_DIM
    cols = lax.broadcasted_iota(jnp.int32, (256, 256), 1) // HEAD_DIM
    return jnp.where(rows == cols, 1.0 / HEAD_DIM, 0.0).astype(BF16)


def head_norm(values, mean_matrix):
    squares = values * values
    high = squares.astype(BF16)
    low = (squares - high.astype(F32)).astype(BF16)
    parts = []
    for start in range(0, values.shape[1], 256):
        cols = slice(start, min(start + 256, values.shape[1]))
        size = cols.stop - start
        matrix = mean_matrix[:size, :size]
        mean = dot(high[:, cols], matrix) + dot(low[:, cols], matrix)
        parts.append((values[:, cols] * lax.rsqrt(mean + EPSILON)).astype(BF16))
    return jnp.concatenate(parts, axis=1)


def first_half(shape):
    return lax.broadcasted_iota(jnp.int32, shape, 1) % PAIR < HEAD_DIM


def row_blocks(n_rows, block, body):
    def step(i, carry):
        body(pl.ds(pl.multiple_of(i * block, block), block))
        return carry

    lax.fori_loop(0, n_rows // block, step, 0)


def project_heads(x_ref, weight, mean_matrix, out_ref, block=512):
    def body(rows):
        out_ref[rows, :] = head_norm(dot(x_ref[rows, :], weight[...]), mean_matrix)

    row_blocks(x_ref.shape[0], block, body)


def project_values(x_ref, weight, out_ref, block=512):
    def body(rows):
        out_ref[rows, :] = dot(x_ref[rows, :], weight[...]).astype(BF16)

    row_blocks(x_ref.shape[0], block, body)


def attend(q_ref, k_ref, v_ref, factor, emit, block=512, unroll=1):
    n_blocks = q_ref.shape[0] // block
    n_steps = n_blocks * (q_ref.shape[1] // PAIR)

    def step(i, carry):
        pair, row = i // n_blocks, i % n_blocks
        cols = pl.ds(pl.multiple_of(pair * PAIR, PAIR), PAIR)
        rows = pl.ds(pl.multiple_of(row * block, block), block)
        queries, keys, values = q_ref[rows, cols], k_ref[:, cols], v_ref[:, cols]
        values = jnp.concatenate([values, jnp.ones_like(values)], axis=1)
        mask = first_half(queries.shape)
        zero = jnp.zeros_like(queries)
        heads = []
        for which in range(2):
            own = (mask, queries, zero) if which == 0 else (mask, zero, queries)
            scores = dot_nt(jnp.where(*own), keys)
            top = jnp.max(scores, axis=1, keepdims=True)
            weights = jnp.exp2((scores - top) * (factor(2 * pair + which) * LOG2E))
            both = dot(weights.astype(BF16), values)
            heads.append((top, both[:, :PAIR], both[:, PAIR:]))
        emit(pair, rows, cols, heads)
        return carry

    lax.fori_loop(0, n_steps, step, 0, unroll=unroll)


def attend_into(q_ref, k_ref, v_ref, scale_ref, stage, out_ref, unroll):
    def emit(pair, rows, cols, heads):
        (_, even, even_total), (_, odd, odd_total) = heads
        mask = first_half(even.shape)
        total = jnp.where(mask, even_total, odd_total)
        inverse = pl.reciprocal(total, approx=True)
        inverse = inverse * (2.0 - total * inverse)
        out_ref[rows, cols] = (jnp.where(mask, even, odd) * inverse).astype(BF16)

    def factor(head):
        return scale_ref[stage, head] / math.sqrt(HEAD_DIM)

    attend(q_ref, k_ref, v_ref, factor, emit, unroll=unroll)


def pack_kernel(read_ref, later_ref, lat_ref, first_ref, rest_ref):
    _, n_rows, width = read_ref.shape
    own_rows = lat_ref.shape[0]
    half = width // CORES
    rest_ref[0] = read_ref[3]
    rest_ref[1:] = later_ref[...]
    lat = lat_ref[...].astype(F32)
    split = own_rows * width // n_rows
    low = own_rows // 2
    extra = jnp.concatenate([lat[:low, split:], lat[low:, split:]], axis=1)
    extra = jnp.concatenate([lat[:, :split], extra], axis=0).astype(BF16)
    for core in range(CORES):
        cols = slice(core * half, (core + 1) * half)
        block = jnp.concatenate([read_ref[i][:, cols] for i in range(3)] + [extra], axis=1)
        first_ref[:, core] = jnp.broadcast_to(block[None], (first_ref.shape[0],) + block.shape)


def unpack_latents(first, own_rows, width):
    devices, n_rows, _ = first.shape
    split = own_rows * width // n_rows
    first = first[:, :, -split:]
    low = first[:, own_rows:]
    low = jnp.concatenate([low[:, :, : split // 2], low[:, :, split // 2 :]], axis=1)
    return jnp.concatenate([first[:, :own_rows], low], axis=2).reshape(devices * own_rows, width)


def read_kernel(
    core_ref,
    scale_ref,
    own_ref,
    peer_ref,
    lat_ref,
    weight_ref,
    out_ref,
    q_ref,
    k_ref,
    v_ref,
    extra_ref,
):
    mean_matrix = head_mean_matrix()
    width = q_ref.shape[1]
    n_heads = width // HEAD_DIM
    n_tok = own_ref.shape[0]
    columns = [pl.ds(i * width, width) for i in range(3)]
    project_heads(lat_ref, weight_ref.at[:, columns[0]], mean_matrix, q_ref)
    for slab, tok_ref in enumerate((own_ref, peer_ref)):
        rows = pl.ds(slab * n_tok, n_tok)
        project_heads(tok_ref, weight_ref.at[:, columns[1]], mean_matrix, k_ref.at[rows, :])
        project_values(tok_ref, weight_ref.at[:, columns[2]], v_ref.at[rows, :])
    extra_ref[...] = jnp.zeros_like(extra_ref)

    def factor(head):
        return scale_ref[0, core_ref[0] * n_heads + head] / math.sqrt(HEAD_DIM)

    def emit(pair, rows, cols, heads):
        (_, even, _), (_, odd, _) = heads
        out_ref[rows, cols] = jnp.where(first_half(even.shape), even, odd).astype(BF16)
        lane = lax.broadcasted_iota(jnp.int32, even.shape, 1)
        extra = extra_ref[rows, :]
        for which, (top, _, total) in enumerate(heads):
            head = 2 * pair + which
            extra = jnp.where(lane == head, top * factor(head), extra)
            extra = jnp.where(lane == TOTALS + head, total, extra)
        extra_ref[rows, :] = extra

    attend(q_ref, k_ref, v_ref, factor, emit, unroll=3)
    extra = extra_ref[...]
    high = extra.astype(BF16).astype(F32)
    mid = (extra - high).astype(BF16).astype(F32)
    low = extra - high - mid
    packed = high + pltpu.roll(mid, PIECE, 1) + pltpu.roll(low, 2 * PIECE, 1)
    out_ref[:, width:] = packed.astype(BF16)


def combine_kernel(part_ref, out_ref, *, parts):
    width = out_ref.shape[-1]
    rows = out_ref.shape[1]
    lane = lax.broadcasted_iota(jnp.int32, (PAIR, width), 0)
    head = lax.broadcasted_iota(jnp.int32, (PAIR, width), 1) // HEAD_DIM
    pick_top = jnp.zeros((PAIR, width), F32)
    pick_total = jnp.zeros((PAIR, width), F32)
    for piece in range(3):
        pick_top = jnp.where(lane == head + piece * PIECE, 1.0, pick_top)
        pick_total = jnp.where(lane == head + TOTALS + piece * PIECE, 1.0, pick_total)
    extra = part_ref[:, width:]
    shape = (parts, rows, width)
    tops = dot(extra, pick_top.astype(BF16)).reshape(shape)
    totals = dot(extra, pick_total.astype(BF16)).reshape(shape)
    rescale = jnp.exp(tops - jnp.max(tops, axis=0, keepdims=True))
    sums = part_ref[:, :width].astype(F32).reshape(shape)
    mixed = jnp.sum(rescale * sums, axis=0) / jnp.sum(rescale * totals, axis=0)
    out_ref[...] = jnp.broadcast_to(mixed.astype(BF16)[None], out_ref.shape)


def query_kernel(tok_ref, weight_ref, out_ref):
    project_heads(tok_ref, weight_ref.at[0], head_mean_matrix(), out_ref)


READ_OUT, SELF_Q, SELF_K, SELF_V, SELF_OUT, WRITE_Q, WRITE_K, WRITE_V, WRITE_OUT = range(9)


def write_kernel(
    index_ref,
    scale_ref,
    mix_ref,
    lat_ref,
    weights_ref,
    raw_hbm_ref,
    query_hbm_ref,
    tok_out_ref,
    lat_out_ref,
    weight_ref,
    raw_ref,
    write_q_ref,
    stream_ref,
    normed_ref,
    q_ref,
    k_ref,
    v_ref,
    att_ref,
    write_att_ref,
    sems,
):
    order = (READ_OUT, SELF_Q, SELF_K, SELF_V, SELF_OUT, WRITE_K, WRITE_V, WRITE_OUT)
    copies = {}
    for slot, matrix in enumerate(order):
        copies[matrix] = pltpu.make_async_copy(
            weights_ref.at[matrix], weight_ref.at[slot], sems.at[slot]
        )
    query_copy = pltpu.make_async_copy(query_hbm_ref, write_q_ref, sems.at[len(order)])
    raw_copy = pltpu.make_async_copy(raw_hbm_ref, raw_ref, sems.at[len(order) + 1])
    for matrix in order:
        copies[matrix].start()
    query_copy.start()
    raw_copy.start()

    def ready(matrix):
        copies[matrix].wait()
        return weight_ref.at[order.index(matrix)]

    mean_matrix = head_mean_matrix()
    n_lat = lat_ref.shape[0]
    own_rows = lat_out_ref.shape[0]
    chips, cores, chip_rows, half = mix_ref.shape
    weight = ready(READ_OUT)
    lat_one = lat_ref[...].astype(F32)
    for core in range(cores):
        mix = mix_ref[:, core].reshape(chips * chip_rows, half)
        lat_one += dot(mix, weight[core * half : (core + 1) * half, :])
    stream_ref[...] = lat_one
    normed_ref[...] = norm_rows(lat_one).astype(BF16)
    project_heads(normed_ref, ready(SELF_Q), mean_matrix, q_ref)
    project_heads(normed_ref, ready(SELF_K), mean_matrix, k_ref)
    project_values(normed_ref, ready(SELF_V), v_ref)
    attend_into(q_ref, k_ref, v_ref, scale_ref, 1, att_ref, 6)
    lat_two = stream_ref[...] + dot(att_ref[...], ready(SELF_OUT)[...])
    stream_ref[...] = lat_two
    normed_ref[...] = norm_rows(lat_two).astype(BF16)
    own = pl.ds(pl.multiple_of(index_ref[0] * own_rows, own_rows), own_rows)
    lat_out_ref[...] = stream_ref[own, :]
    project_heads(normed_ref, ready(WRITE_K), mean_matrix, k_ref)
    project_values(normed_ref, ready(WRITE_V), v_ref)
    query_copy.wait()
    attend_into(write_q_ref, k_ref, v_ref, scale_ref, 2, write_att_ref, 4)
    weight = ready(WRITE_OUT)
    raw_copy.wait()

    def last(rows):
        update = dot(write_att_ref[rows, :], weight[...])
        tok_out_ref[rows, :] = (raw_ref[rows, :].astype(F32) + update).astype(BF16)

    row_blocks(raw_ref.shape[0], 512, last)


IN_VMEM = pl.BlockSpec(memory_space=pltpu.VMEM)
IN_SMEM = pl.BlockSpec(memory_space=pltpu.SMEM)
IN_PLACE = pl.BlockSpec(memory_space=pl.ANY)


def shards(tokens, latents, read_weights, later_weights, head_scale):
    n_tok, width = tokens.shape
    own_rows = latents.shape[0]
    devices = lax.axis_size("seq")
    chips = devices // CORES
    n_lat = own_rows * devices
    half = width // CORES
    weight_rows = read_weights.shape[1]
    index = lax.axis_index("seq").astype(jnp.int32)
    same_core = [[CORES * chip + core for chip in range(chips)] for core in range(CORES)]
    swap = [(device, device ^ 1) for device in range(devices)]

    params = pltpu.CompilerParams(vmem_limit_bytes=VMEM_LIMIT)
    packed_width = 3 * half + own_rows * width // weight_rows
    first, rest = pl.pallas_call(
        pack_kernel,
        name="pack",
        out_shape=(
            jax.ShapeDtypeStruct((chips, CORES, weight_rows, packed_width), BF16),
            jax.ShapeDtypeStruct((9, weight_rows, width), BF16),
        ),
        in_specs=[IN_VMEM] * 3,
        out_specs=(IN_VMEM, IN_VMEM),
        compiler_params=params,
    )(read_weights, later_weights, latents)
    first = first.reshape(devices, weight_rows, packed_width)
    first = lax.all_to_all(first, "seq", 0, 0, tiled=True)
    lat_full = unpack_latents(first, own_rows, width)
    first = first.reshape(width, packed_width)
    rest = lax.all_gather(rest, "seq", axis=1, tiled=True)
    tok_normed = norm_rows(tokens).astype(BF16)
    peer_normed = lax.ppermute(tok_normed, "seq", swap)
    lat_normed = norm_rows(lat_full).astype(BF16)
    parts = pl.pallas_call(
        read_kernel,
        name="read",
        out_shape=jax.ShapeDtypeStruct((n_lat, half + PAIR), BF16),
        in_specs=[IN_SMEM, IN_SMEM] + [IN_VMEM] * 4,
        out_specs=IN_VMEM,
        scratch_shapes=[
            pltpu.VMEM((n_lat, half), BF16),
            pltpu.VMEM((2 * n_tok, half), BF16),
            pltpu.VMEM((2 * n_tok, half), BF16),
            pltpu.VMEM((n_lat, PAIR), F32),
        ],
        compiler_params=params,
        cost_estimate=pl.CostEstimate(
            flops=20_000_000_000, bytes_accessed=8_000_000, transcendentals=6_300_000
        ),
    )((index % CORES).reshape(1), head_scale, tok_normed, peer_normed, lat_normed, first)
    queries = pl.pallas_call(
        query_kernel,
        name="query",
        grid=(1,),
        out_shape=jax.ShapeDtypeStruct((n_tok, width), BF16),
        in_specs=[
            pl.BlockSpec((n_tok, width), lambda i: (0, 0)),
            pl.BlockSpec((1, width, width), lambda i: (WRITE_Q, 0, 0)),
        ],
        out_specs=pl.BlockSpec((n_tok, width), lambda i: (0, 0)),
        compiler_params=params,
        cost_estimate=pl.CostEstimate(
            flops=4_000_000_000, bytes_accessed=5_000_000, transcendentals=800_000
        ),
    )(tok_normed, rest)
    parts = lax.all_to_all(
        parts.reshape(chips, CORES * own_rows, half + PAIR),
        "seq",
        0,
        0,
        tiled=True,
        axis_index_groups=same_core,
    )
    mixed = pl.pallas_call(
        functools.partial(combine_kernel, parts=chips),
        name="combine",
        out_shape=jax.ShapeDtypeStruct((devices, CORES * own_rows, half), BF16),
        in_specs=[IN_VMEM],
        out_specs=IN_VMEM,
        compiler_params=params,
    )(parts.reshape(n_lat, half + PAIR))
    mixed = lax.all_to_all(mixed, "seq", 0, 0, tiled=True)
    mixed = mixed.reshape(chips, CORES, CORES * own_rows, half)
    latents_bf16 = pltpu.VMEM((n_lat, width), BF16)
    tokens_bf16 = pltpu.VMEM((n_tok, width), BF16)
    return pl.pallas_call(
        write_kernel,
        name="write",
        out_shape=(
            jax.ShapeDtypeStruct(tokens.shape, BF16),
            jax.ShapeDtypeStruct(latents.shape, F32),
        ),
        in_specs=[IN_SMEM, IN_SMEM, IN_VMEM, IN_VMEM, IN_PLACE, IN_PLACE, IN_PLACE],
        out_specs=(IN_VMEM, IN_VMEM),
        scratch_shapes=[
            pltpu.VMEM((8, width, width), BF16),
            tokens_bf16,
            tokens_bf16,
            pltpu.VMEM((n_lat, width), F32),
            latents_bf16,
            latents_bf16,
            latents_bf16,
            latents_bf16,
            latents_bf16,
            tokens_bf16,
            pltpu.SemaphoreType.DMA((10,)),
        ],
        compiler_params=params,
    )(index.reshape(1), head_scale, mixed, lat_full, rest, tokens, queries)


def solution(mesh):
    placed = (
        P(("vid", "seq"), None),
        P(("vid", "seq"), None),
        P(None, "seq", None),
        P(None, "seq", None),
        P(),
    )
    return jax.shard_map(
        shards,
        mesh=mesh,
        in_specs=placed,
        out_specs=(P(("vid", "seq"), None), P(("vid", "seq"), None)),
        check_vma=False,
    )
```

```python
import functools
import math

import jax
import jax.numpy as jnp
from jax import lax
from jax.experimental import pallas as pl
from jax.experimental.pallas import tpu as pltpu
from jax.sharding import PartitionSpec as P

HEADS = 12
HEAD_DIM = 64
PAIR = 2 * HEAD_DIM
EPSILON = 1e-06
LOG2E = math.log2(math.e)
BF16 = jnp.bfloat16
F32 = jnp.float32
MIB = 1024 * 1024
PACK_VMEM = 58 * MIB
READ_VMEM = 40 * MIB
COMBINE_VMEM = 40 * MIB
QUERY_VMEM = 50 * MIB
WRITE_VMEM = 50 * MIB
PIECE = 16
TOTALS = 6
CORES = 2
WRITE_UNROLL = 12


def norm_rows(values):
    values = values.astype(F32)
    return values * lax.rsqrt(jnp.mean(values * values, axis=-1, keepdims=True) + EPSILON)


def dot(left, right):
    return jnp.dot(left, right, preferred_element_type=F32)


def dot_nt(left, right):
    return lax.dot_general(left, right, (((1,), (1,)), ((), ())), preferred_element_type=F32)


def head_mean_matrix():
    rows = lax.broadcasted_iota(jnp.int32, (256, 256), 0) // HEAD_DIM
    cols = lax.broadcasted_iota(jnp.int32, (256, 256), 1) // HEAD_DIM
    return jnp.where(rows == cols, 1.0 / HEAD_DIM, 0.0).astype(BF16)


def head_norm(values, mean_matrix):
    squares = values * values
    high = squares.astype(BF16)
    low = (squares - high.astype(F32)).astype(BF16)
    parts = []
    for start in range(0, values.shape[1], 256):
        cols = slice(start, min(start + 256, values.shape[1]))
        size = cols.stop - start
        matrix = mean_matrix[:size, :size]
        mean = dot(high[:, cols], matrix) + dot(low[:, cols], matrix)
        parts.append((values[:, cols] * lax.rsqrt(mean + EPSILON)).astype(BF16))
    return jnp.concatenate(parts, axis=1)


def first_half(shape):
    return lax.broadcasted_iota(jnp.int32, shape, 1) % PAIR < HEAD_DIM


def row_blocks(n_rows, block, body):
    for start in range(0, n_rows, block):
        body(pl.ds(start, block))


def project_heads(x_ref, weight, mean_matrix, out_ref, block=512):
    def body(rows):
        out_ref[rows, :] = head_norm(dot(x_ref[rows, :], weight[...]), mean_matrix)

    row_blocks(x_ref.shape[0], block, body)


def project_values(x_ref, weight, out_ref, block=512):
    def body(rows):
        out_ref[rows, :] = dot(x_ref[rows, :], weight[...]).astype(BF16)

    row_blocks(x_ref.shape[0], block, body)


def attend(q_ref, k_ref, v_ref, factor, emit, block=512, unroll=1):
    n_blocks = q_ref.shape[0] // block
    n_steps = n_blocks * (q_ref.shape[1] // PAIR)

    def step(i, carry):
        pair, row = i // n_blocks, i % n_blocks
        cols, rows = pair * PAIR, row * block
        if not isinstance(i, int):
            cols, rows = pl.multiple_of(cols, PAIR), pl.multiple_of(rows, block)
        cols, rows = pl.ds(cols, PAIR), pl.ds(rows, block)
        queries, keys, values = q_ref[rows, cols], k_ref[:, cols], v_ref[:, cols]
        values = jnp.concatenate([values, jnp.ones_like(values)], axis=1)
        mask = first_half(queries.shape)
        zero = jnp.zeros_like(queries)
        heads = []
        for which in range(2):
            own = (mask, queries, zero) if which == 0 else (mask, zero, queries)
            scores = dot_nt(jnp.where(*own), keys)
            top = jnp.max(scores, axis=1, keepdims=True)
            weights = jnp.exp2((scores - top) * (factor(2 * pair + which) * LOG2E))
            both = dot(weights.astype(BF16), values)
            heads.append((top, both[:, :PAIR], both[:, PAIR:]))
        emit(pair, rows, cols, heads)
        return carry

    if unroll >= n_steps:
        for i in range(n_steps):
            step(i, 0)
    else:
        lax.fori_loop(0, n_steps, step, 0, unroll=unroll)


def attend_into(q_ref, k_ref, v_ref, scale_ref, stage, out_ref, unroll):
    def emit(pair, rows, cols, heads):
        (_, even, even_total), (_, odd, odd_total) = heads
        mask = first_half(even.shape)
        total = jnp.where(mask, even_total, odd_total)
        inverse = pl.reciprocal(total, approx=True)
        inverse = inverse * (2.0 - total * inverse)
        out_ref[rows, cols] = (jnp.where(mask, even, odd) * inverse).astype(BF16)

    def factor(head):
        return scale_ref[stage, head] / math.sqrt(HEAD_DIM)

    attend(q_ref, k_ref, v_ref, factor, emit, unroll=unroll)


def pack_kernel(read_ref, later_ref, lat_ref, first_ref, rest_ref):
    _, n_rows, width = read_ref.shape
    own_rows = lat_ref.shape[0]
    half = width // CORES
    rest_ref[0] = read_ref[3]
    rest_ref[1:] = later_ref[...]
    lat = lat_ref[...].astype(F32)
    split = own_rows * width // n_rows
    low = own_rows // 2
    extra = jnp.concatenate([lat[:low, split:], lat[low:, split:]], axis=1)
    extra = jnp.concatenate([lat[:, :split], extra], axis=0).astype(BF16)
    for core in range(CORES):
        cols = slice(core * half, (core + 1) * half)
        block = jnp.concatenate([read_ref[i][:, cols] for i in range(3)] + [extra], axis=1)
        first_ref[:, core] = jnp.broadcast_to(block[None], (first_ref.shape[0],) + block.shape)


def unpack_latents(blocks, own_rows, width):
    devices, n_rows, split = blocks.shape
    blocks = blocks.astype(F32)
    low = blocks[:, own_rows:]
    low = jnp.concatenate([low[:, :, : split // 2], low[:, :, split // 2 :]], axis=1)
    high = blocks[:, :own_rows].reshape(devices * own_rows, split)
    return jnp.concatenate([high, low.reshape(devices * own_rows, width - split)], axis=1)


def read_kernel(
    core_ref,
    scale_ref,
    own_hbm_ref,
    peer_hbm_ref,
    first_hbm_ref,
    block_hbm_ref,
    out_ref,
    lat_ref,
    own_ref,
    peer_ref,
    weight_ref,
    block_ref,
    normed_ref,
    q_ref,
    k_ref,
    v_ref,
    extra_ref,
    sems,
):
    width = q_ref.shape[1]
    columns = [pl.ds(i * width, width) for i in range(3)]
    block_copy = pltpu.make_async_copy(
        block_hbm_ref.at[:, :, pl.ds(3 * width, block_ref.shape[2])], block_ref, sems.at[0]
    )
    weight_copies = [
        pltpu.make_async_copy(
            first_hbm_ref.at[:, columns[i]], weight_ref.at[:, columns[i]], sems.at[1 + i]
        )
        for i in range(3)
    ]
    own_copy = pltpu.make_async_copy(own_hbm_ref, own_ref, sems.at[4])
    peer_copy = pltpu.make_async_copy(peer_hbm_ref, peer_ref, sems.at[5])
    for copy in (block_copy, weight_copies[0], own_copy, *weight_copies[1:], peer_copy):
        copy.start()
    mean_matrix = head_mean_matrix()
    n_heads = width // HEAD_DIM
    n_tok = own_ref.shape[0]
    n_lat, full_width = lat_ref.shape
    block_copy.wait()
    lat = unpack_latents(block_ref[...], n_lat // block_ref.shape[0], full_width)
    lat_ref[...] = lat.astype(BF16)
    normed_ref[...] = norm_rows(lat).astype(BF16)
    weight_copies[0].wait()
    project_heads(normed_ref, weight_ref.at[:, columns[0]], mean_matrix, q_ref)
    own_copy.wait()
    for slab, tok_ref in enumerate((own_ref, peer_ref)):
        rows = pl.ds(slab * n_tok, n_tok)
        if slab == 0:
            weight_copies[1].wait()
        else:
            peer_copy.wait()
        project_heads(tok_ref, weight_ref.at[:, columns[1]], mean_matrix, k_ref.at[rows, :])
        if slab == 0:
            weight_copies[2].wait()
        project_values(tok_ref, weight_ref.at[:, columns[2]], v_ref.at[rows, :])
    extra_ref[...] = jnp.zeros_like(extra_ref)

    def factor(head):
        return scale_ref[0, core_ref[0] * n_heads + head] / math.sqrt(HEAD_DIM)

    def emit(pair, rows, cols, heads):
        (_, even, _), (_, odd, _) = heads
        out_ref[rows, cols] = jnp.where(first_half(even.shape), even, odd).astype(BF16)
        lane = lax.broadcasted_iota(jnp.int32, even.shape, 1)
        extra = extra_ref[rows, :]
        for which, (top, _, total) in enumerate(heads):
            head = 2 * pair + which
            extra = jnp.where(lane == head, top * factor(head), extra)
            extra = jnp.where(lane == TOTALS + head, total, extra)
        extra_ref[rows, :] = extra

    attend(q_ref, k_ref, v_ref, factor, emit, unroll=3)
    extra = extra_ref[...]
    high = extra.astype(BF16).astype(F32)
    mid = (extra - high).astype(BF16).astype(F32)
    low = extra - high - mid
    packed = high + pltpu.roll(mid, PIECE, 1) + pltpu.roll(low, 2 * PIECE, 1)
    out_ref[:, width:] = packed.astype(BF16)


def combine_kernel(part_ref, out_ref, *, parts):
    width = out_ref.shape[-1]
    rows = out_ref.shape[1]
    lane = lax.broadcasted_iota(jnp.int32, (PAIR, width), 0)
    head = lax.broadcasted_iota(jnp.int32, (PAIR, width), 1) // HEAD_DIM
    pick_top = jnp.zeros((PAIR, width), F32)
    pick_total = jnp.zeros((PAIR, width), F32)
    for piece in range(3):
        pick_top = jnp.where(lane == head + piece * PIECE, 1.0, pick_top)
        pick_total = jnp.where(lane == head + TOTALS + piece * PIECE, 1.0, pick_total)
    extra = part_ref[:, width:]
    shape = (parts, rows, width)
    tops = dot(extra, pick_top.astype(BF16)).reshape(shape)
    totals = dot(extra, pick_total.astype(BF16)).reshape(shape)
    rescale = jnp.exp(tops - jnp.max(tops, axis=0, keepdims=True))
    sums = part_ref[:, :width].astype(F32).reshape(shape)
    mixed = jnp.sum(rescale * sums, axis=0) / jnp.sum(rescale * totals, axis=0)
    out_ref[...] = jnp.broadcast_to(mixed.astype(BF16)[None], out_ref.shape)


def query_kernel(tok_ref, weight_ref, out_ref):
    project_heads(tok_ref, weight_ref.at[0], head_mean_matrix(), out_ref)


READ_OUT, SELF_Q, SELF_K, SELF_V, SELF_OUT, WRITE_Q, WRITE_K, WRITE_V, WRITE_OUT = range(9)


def write_kernel(
    index_ref,
    scale_ref,
    mix_ref,
    lat_ref,
    weights_ref,
    raw_hbm_ref,
    query_hbm_ref,
    tok_out_ref,
    lat_out_ref,
    weight_ref,
    raw_ref,
    write_q_ref,
    stream_ref,
    normed_ref,
    q_ref,
    k_ref,
    v_ref,
    att_ref,
    write_att_ref,
    sems,
):
    order = (READ_OUT, SELF_Q, SELF_K, SELF_V, SELF_OUT, WRITE_K, WRITE_V, WRITE_OUT)
    copies = {}
    for slot, matrix in enumerate(order):
        copies[matrix] = pltpu.make_async_copy(
            weights_ref.at[matrix], weight_ref.at[slot], sems.at[slot]
        )
    query_copy = pltpu.make_async_copy(query_hbm_ref, write_q_ref, sems.at[len(order)])
    raw_copy = pltpu.make_async_copy(raw_hbm_ref, raw_ref, sems.at[len(order) + 1])
    for matrix in order:
        copies[matrix].start()
    query_copy.start()
    raw_copy.start()

    def ready(matrix):
        copies[matrix].wait()
        return weight_ref.at[order.index(matrix)]

    mean_matrix = head_mean_matrix()
    n_lat = lat_ref.shape[0]
    own_rows = lat_out_ref.shape[0]
    chips, cores, chip_rows, half = mix_ref.shape
    weight = ready(READ_OUT)
    lat_one = lat_ref[...].astype(F32)
    for core in range(cores):
        mix = mix_ref[:, core].reshape(chips * chip_rows, half)
        lat_one += dot(mix, weight[core * half : (core + 1) * half, :])
    stream_ref[...] = lat_one
    normed_ref[...] = norm_rows(lat_one).astype(BF16)
    project_heads(normed_ref, ready(SELF_Q), mean_matrix, q_ref)
    project_heads(normed_ref, ready(SELF_K), mean_matrix, k_ref)
    project_values(normed_ref, ready(SELF_V), v_ref)
    attend_into(q_ref, k_ref, v_ref, scale_ref, 1, att_ref, 6)
    lat_two = stream_ref[...] + dot(att_ref[...], ready(SELF_OUT)[...])
    stream_ref[...] = lat_two
    normed_ref[...] = norm_rows(lat_two).astype(BF16)
    own = pl.ds(pl.multiple_of(index_ref[0] * own_rows, own_rows), own_rows)
    lat_out_ref[...] = stream_ref[own, :]
    project_heads(normed_ref, ready(WRITE_K), mean_matrix, k_ref)
    project_values(normed_ref, ready(WRITE_V), v_ref)
    query_copy.wait()
    attend_into(write_q_ref, k_ref, v_ref, scale_ref, 2, write_att_ref, WRITE_UNROLL)
    weight = ready(WRITE_OUT)
    raw_copy.wait()

    def last(rows):
        update = dot(write_att_ref[rows, :], weight[...])
        tok_out_ref[rows, :] = (raw_ref[rows, :].astype(F32) + update).astype(BF16)

    row_blocks(raw_ref.shape[0], 512, last)


IN_VMEM = pl.BlockSpec(memory_space=pltpu.VMEM)
IN_SMEM = pl.BlockSpec(memory_space=pltpu.SMEM)
IN_PLACE = pl.BlockSpec(memory_space=pl.ANY)


def read_call(core, head_scale, own, peer, blocks, n_lat):
    n_tok, width = own.shape
    half = width // CORES
    devices, n_rows, packed_width = blocks.shape
    tokens_bf16 = pltpu.VMEM((n_tok, width), BF16)
    return pl.pallas_call(
        read_kernel,
        name="read",
        out_shape=(
            jax.ShapeDtypeStruct((n_lat, half + PAIR), BF16),
            jax.ShapeDtypeStruct((n_lat, width), BF16),
        ),
        in_specs=[IN_SMEM, IN_SMEM] + [IN_PLACE] * 4,
        out_specs=(IN_VMEM, IN_VMEM),
        scratch_shapes=[
            tokens_bf16,
            tokens_bf16,
            pltpu.VMEM((width, 3 * half), BF16),
            pltpu.VMEM((devices, n_rows, packed_width - 3 * half), BF16),
            pltpu.VMEM((n_lat, width), BF16),
            pltpu.VMEM((n_lat, half), BF16),
            pltpu.VMEM((2 * n_tok, half), BF16),
            pltpu.VMEM((2 * n_tok, half), BF16),
            pltpu.VMEM((n_lat, PAIR), F32),
            pltpu.SemaphoreType.DMA((6,)),
        ],
        compiler_params=pltpu.CompilerParams(vmem_limit_bytes=READ_VMEM),
        cost_estimate=pl.CostEstimate(
            flops=20_000_000_000, bytes_accessed=8_000_000, transcendentals=6_300_000
        ),
    )(core, head_scale, own, peer, blocks.reshape(devices * n_rows, packed_width), blocks)


def write_call(index, head_scale, mixed, lat_full, rest, tokens, queries, own_rows):
    n_lat, width = lat_full.shape
    latents_bf16 = pltpu.VMEM((n_lat, width), BF16)
    tokens_bf16 = pltpu.VMEM(tokens.shape, BF16)
    return pl.pallas_call(
        write_kernel,
        name="write",
        out_shape=(
            jax.ShapeDtypeStruct(tokens.shape, BF16),
            jax.ShapeDtypeStruct((own_rows, width), F32),
        ),
        in_specs=[IN_SMEM, IN_SMEM, IN_VMEM, IN_VMEM, IN_PLACE, IN_PLACE, IN_PLACE],
        out_specs=(IN_VMEM, IN_VMEM),
        scratch_shapes=[
            pltpu.VMEM((8, width, width), BF16),
            tokens_bf16,
            tokens_bf16,
            pltpu.VMEM((n_lat, width), F32),
            latents_bf16,
            latents_bf16,
            latents_bf16,
            latents_bf16,
            latents_bf16,
            tokens_bf16,
            pltpu.SemaphoreType.DMA((10,)),
        ],
        compiler_params=pltpu.CompilerParams(vmem_limit_bytes=WRITE_VMEM),
    )(index, head_scale, mixed, lat_full, rest, tokens, queries)


def shards(tokens, latents, read_weights, later_weights, head_scale):
    n_tok, width = tokens.shape
    own_rows = latents.shape[0]
    devices = lax.axis_size("seq")
    chips = devices // CORES
    n_lat = own_rows * devices
    half = width // CORES
    weight_rows = read_weights.shape[1]
    index = lax.axis_index("seq").astype(jnp.int32)
    same_core = [[CORES * chip + core for chip in range(chips)] for core in range(CORES)]
    swap = [(device, device ^ 1) for device in range(devices)]

    packed_width = 3 * half + own_rows * width // weight_rows
    first, rest = pl.pallas_call(
        pack_kernel,
        name="pack",
        out_shape=(
            jax.ShapeDtypeStruct((chips, CORES, weight_rows, packed_width), BF16),
            jax.ShapeDtypeStruct((9, weight_rows, width), BF16),
        ),
        in_specs=[IN_VMEM] * 3,
        out_specs=(IN_VMEM, IN_VMEM),
        compiler_params=pltpu.CompilerParams(vmem_limit_bytes=PACK_VMEM),
    )(read_weights, later_weights, latents)
    first = first.reshape(devices, weight_rows, packed_width)
    first = lax.all_to_all(first, "seq", 0, 0, tiled=True)
    rest = lax.all_gather(rest, "seq", axis=1, tiled=True)
    tok_normed = norm_rows(tokens).astype(BF16)
    peer_normed = lax.ppermute(tok_normed, "seq", swap)
    parts, lat_full = read_call(
        (index % CORES).reshape(1), head_scale, tok_normed, peer_normed, first, n_lat
    )
    queries = pl.pallas_call(
        query_kernel,
        name="query",
        grid=(1,),
        out_shape=jax.ShapeDtypeStruct((n_tok, width), BF16),
        in_specs=[
            pl.BlockSpec((n_tok, width), lambda i: (0, 0)),
            pl.BlockSpec((1, width, width), lambda i: (WRITE_Q, 0, 0)),
        ],
        out_specs=pl.BlockSpec((n_tok, width), lambda i: (0, 0)),
        compiler_params=pltpu.CompilerParams(vmem_limit_bytes=QUERY_VMEM),
        cost_estimate=pl.CostEstimate(
            flops=4_000_000_000, bytes_accessed=5_000_000, transcendentals=800_000
        ),
    )(tok_normed, rest)
    parts = lax.all_to_all(
        parts.reshape(chips, CORES * own_rows, half + PAIR),
        "seq",
        0,
        0,
        tiled=True,
        axis_index_groups=same_core,
    )
    mixed = pl.pallas_call(
        functools.partial(combine_kernel, parts=chips),
        name="combine",
        out_shape=jax.ShapeDtypeStruct((devices, CORES * own_rows, half), BF16),
        in_specs=[IN_VMEM],
        out_specs=IN_VMEM,
        compiler_params=pltpu.CompilerParams(vmem_limit_bytes=COMBINE_VMEM),
    )(parts.reshape(n_lat, half + PAIR))
    mixed = lax.all_to_all(mixed, "seq", 0, 0, tiled=True)
    mixed = mixed.reshape(chips, CORES, CORES * own_rows, half)
    return write_call(
        index.reshape(1), head_scale, mixed, lat_full, rest, tokens, queries, own_rows
    )


def solution(mesh):
    placed = (
        P(("vid", "seq"), None),
        P(("vid", "seq"), None),
        P(None, "seq", None),
        P(None, "seq", None),
        P(),
    )
    return jax.shard_map(
        shards,
        mesh=mesh,
        in_specs=placed,
        out_specs=(P(("vid", "seq"), None), P(("vid", "seq"), None)),
        check_vma=False,
    )
```

```python
import functools
import math

import jax
import jax.numpy as jnp
from jax import lax
from jax.experimental import pallas as pl
from jax.experimental.pallas import tpu as pltpu
from jax.sharding import PartitionSpec as P

HEADS = 12
HEAD_DIM = 64
PAIR = 2 * HEAD_DIM
EPSILON = 1e-06
LOG2E = math.log2(math.e)
BF16 = jnp.bfloat16
F32 = jnp.float32
MIB = 1024 * 1024
PACK_VMEM = 58 * MIB
READ_VMEM = 56 * MIB
COMBINE_VMEM = 40 * MIB
QUERY_VMEM = 50 * MIB
WRITE_VMEM = 50 * MIB
PIECE = 16
TOTALS = 6
CORES = 2
WRITE_UNROLL = 4


def norm_rows(values):
    values = values.astype(F32)
    return values * lax.rsqrt(jnp.mean(values * values, axis=-1, keepdims=True) + EPSILON)


def dot(left, right):
    return jnp.dot(left, right, preferred_element_type=F32)


def dot_nt(left, right):
    return lax.dot_general(left, right, (((1,), (1,)), ((), ())), preferred_element_type=F32)


def head_mean_matrix():
    rows = lax.broadcasted_iota(jnp.int32, (256, 256), 0) // HEAD_DIM
    cols = lax.broadcasted_iota(jnp.int32, (256, 256), 1) // HEAD_DIM
    return jnp.where(rows == cols, 1.0 / HEAD_DIM, 0.0).astype(BF16)


def head_norm(values, mean_matrix):
    squares = values * values
    high = squares.astype(BF16)
    low = (squares - high.astype(F32)).astype(BF16)
    parts = []
    for start in range(0, values.shape[1], 256):
        cols = slice(start, min(start + 256, values.shape[1]))
        size = cols.stop - start
        matrix = mean_matrix[:size, :size]
        mean = dot(high[:, cols], matrix) + dot(low[:, cols], matrix)
        parts.append((values[:, cols] * lax.rsqrt(mean + EPSILON)).astype(BF16))
    return jnp.concatenate(parts, axis=1)


def first_half(shape):
    return lax.broadcasted_iota(jnp.int32, shape, 1) % PAIR < HEAD_DIM


def row_blocks(n_rows, block, body):
    for start in range(0, n_rows, block):
        body(pl.ds(start, block))


def project_heads(x_ref, weight, mean_matrix, out_ref, block=512):
    def body(rows):
        out_ref[rows, :] = head_norm(dot(x_ref[rows, :], weight[...]), mean_matrix)

    row_blocks(x_ref.shape[0], block, body)


def project_values(x_ref, weight, out_ref, block=512):
    def body(rows):
        out_ref[rows, :] = dot(x_ref[rows, :], weight[...]).astype(BF16)

    row_blocks(x_ref.shape[0], block, body)


def attend(q_ref, k_ref, v_ref, factor, emit, block=512, unroll=1):
    n_blocks = q_ref.shape[0] // block
    n_steps = n_blocks * (q_ref.shape[1] // PAIR)

    def step(i, carry):
        pair, row = i // n_blocks, i % n_blocks
        cols, rows = pair * PAIR, row * block
        if not isinstance(i, int):
            cols, rows = pl.multiple_of(cols, PAIR), pl.multiple_of(rows, block)
        cols, rows = pl.ds(cols, PAIR), pl.ds(rows, block)
        queries, keys, values = q_ref[rows, cols], k_ref[:, cols], v_ref[:, cols]
        values = jnp.concatenate([values, jnp.ones_like(values)], axis=1)
        mask = first_half(queries.shape)
        zero = jnp.zeros_like(queries)
        heads = []
        for which in range(2):
            own = (mask, queries, zero) if which == 0 else (mask, zero, queries)
            scores = dot_nt(jnp.where(*own), keys)
            top = jnp.max(scores, axis=1, keepdims=True)
            weights = jnp.exp2((scores - top) * (factor(2 * pair + which) * LOG2E))
            both = dot(weights.astype(BF16), values)
            heads.append((top, both[:, :PAIR], both[:, PAIR:]))
        emit(pair, rows, cols, heads)
        return carry

    if unroll >= n_steps:
        for i in range(n_steps):
            step(i, 0)
    else:
        lax.fori_loop(0, n_steps, step, 0, unroll=unroll)


def attend_into(q_ref, k_ref, v_ref, scale_ref, stage, out_ref, unroll):
    def emit(pair, rows, cols, heads):
        (_, even, even_total), (_, odd, odd_total) = heads
        mask = first_half(even.shape)
        total = jnp.where(mask, even_total, odd_total)
        inverse = pl.reciprocal(total, approx=True)
        inverse = inverse * (2.0 - total * inverse)
        out_ref[rows, cols] = (jnp.where(mask, even, odd) * inverse).astype(BF16)

    def factor(head):
        return scale_ref[stage, head] / math.sqrt(HEAD_DIM)

    attend(q_ref, k_ref, v_ref, factor, emit, unroll=unroll)


def pack_kernel(read_ref, later_ref, lat_ref, first_ref, rest_ref):
    _, n_rows, width = read_ref.shape
    own_rows = lat_ref.shape[0]
    half = width // CORES
    rest_ref[0] = read_ref[3]
    rest_ref[1:] = later_ref[...]
    lat = lat_ref[...].astype(F32)
    split = own_rows * width // n_rows
    low = own_rows // 2
    extra = jnp.concatenate([lat[:low, split:], lat[low:, split:]], axis=1)
    extra = jnp.concatenate([lat[:, :split], extra], axis=0).astype(BF16)
    for core in range(CORES):
        cols = slice(core * half, (core + 1) * half)
        block = jnp.concatenate([read_ref[i][:, cols] for i in range(3)] + [extra], axis=1)
        first_ref[:, core] = jnp.broadcast_to(block[None], (first_ref.shape[0],) + block.shape)


def unpack_latents(blocks, own_rows, width):
    devices, n_rows, split = blocks.shape
    blocks = blocks.astype(F32)
    low = blocks[:, own_rows:]
    low = jnp.concatenate([low[:, :, : split // 2], low[:, :, split // 2 :]], axis=1)
    high = blocks[:, :own_rows].reshape(devices * own_rows, split)
    return jnp.concatenate([high, low.reshape(devices * own_rows, width - split)], axis=1)


def read_kernel(
    core_ref,
    scale_ref,
    own_hbm_ref,
    peer_hbm_ref,
    first_hbm_ref,
    block_hbm_ref,
    out_ref,
    lat_ref,
    tok_ref,
    weight_ref,
    block_ref,
    normed_ref,
    q_ref,
    k_ref,
    v_ref,
    extra_ref,
    sems,
):
    width = q_ref.shape[1]
    columns = [pl.ds(i * width, width) for i in range(3)]
    block_copy = pltpu.make_async_copy(
        block_hbm_ref.at[:, :, pl.ds(3 * width, block_ref.shape[2])], block_ref, sems.at[0]
    )
    weight_copies = [
        pltpu.make_async_copy(
            first_hbm_ref.at[:, columns[i]], weight_ref.at[:, columns[i]], sems.at[1 + i]
        )
        for i in range(3)
    ]
    n_tok = own_hbm_ref.shape[0]
    own_copy = pltpu.make_async_copy(own_hbm_ref, tok_ref.at[pl.ds(0, n_tok), :], sems.at[4])
    peer_copy = pltpu.make_async_copy(
        peer_hbm_ref, tok_ref.at[pl.ds(n_tok, n_tok), :], sems.at[5]
    )
    for copy in (block_copy, weight_copies[0], own_copy, *weight_copies[1:], peer_copy):
        copy.start()
    mean_matrix = head_mean_matrix()
    n_heads = width // HEAD_DIM
    n_lat, full_width = lat_ref.shape
    block_copy.wait()
    lat = unpack_latents(block_ref[...], n_lat // block_ref.shape[0], full_width)
    lat_ref[...] = lat.astype(BF16)
    normed_ref[...] = norm_rows(lat).astype(BF16)
    weight_copies[0].wait()
    project_heads(normed_ref, weight_ref.at[:, columns[0]], mean_matrix, q_ref)
    own_copy.wait()
    for copy in (*weight_copies[1:], peer_copy):
        copy.wait()

    def project_block(i, carry):
        rows = pl.ds(pl.multiple_of(i * 512, 512), 512)
        keys = dot(tok_ref[rows, :], weight_ref[:, columns[1]])
        k_ref[rows, :] = head_norm(keys, mean_matrix)
        v_ref[rows, :] = dot(tok_ref[rows, :], weight_ref[:, columns[2]]).astype(BF16)
        return carry

    lax.fori_loop(0, tok_ref.shape[0] // 512, project_block, 0)
    extra_ref[...] = jnp.zeros_like(extra_ref)

    def factor(head):
        return scale_ref[0, core_ref[0] * n_heads + head] / math.sqrt(HEAD_DIM)

    def emit(pair, rows, cols, heads):
        (_, even, _), (_, odd, _) = heads
        out_ref[rows, cols] = jnp.where(first_half(even.shape), even, odd).astype(BF16)
        lane = lax.broadcasted_iota(jnp.int32, even.shape, 1)
        extra = extra_ref[rows, :]
        for which, (top, _, total) in enumerate(heads):
            head = 2 * pair + which
            extra = jnp.where(lane == head, top * factor(head), extra)
            extra = jnp.where(lane == TOTALS + head, total, extra)
        extra_ref[rows, :] = extra

    attend(q_ref, k_ref, v_ref, factor, emit, unroll=3)
    extra = extra_ref[...]
    high = extra.astype(BF16).astype(F32)
    mid = (extra - high).astype(BF16).astype(F32)
    low = extra - high - mid
    packed = high + pltpu.roll(mid, PIECE, 1) + pltpu.roll(low, 2 * PIECE, 1)
    out_ref[:, width:] = packed.astype(BF16)


def combine_kernel(part_ref, out_ref, *, parts):
    width = out_ref.shape[-1]
    rows = out_ref.shape[1]
    lane = lax.broadcasted_iota(jnp.int32, (PAIR, width), 0)
    head = lax.broadcasted_iota(jnp.int32, (PAIR, width), 1) // HEAD_DIM
    pick_top = jnp.zeros((PAIR, width), F32)
    pick_total = jnp.zeros((PAIR, width), F32)
    for piece in range(3):
        pick_top = jnp.where(lane == head + piece * PIECE, 1.0, pick_top)
        pick_total = jnp.where(lane == head + TOTALS + piece * PIECE, 1.0, pick_total)
    extra = part_ref[:, width:]
    shape = (parts, rows, width)
    tops = dot(extra, pick_top.astype(BF16)).reshape(shape)
    totals = dot(extra, pick_total.astype(BF16)).reshape(shape)
    rescale = jnp.exp(tops - jnp.max(tops, axis=0, keepdims=True))
    sums = part_ref[:, :width].astype(F32).reshape(shape)
    mixed = jnp.sum(rescale * sums, axis=0) / jnp.sum(rescale * totals, axis=0)
    out_ref[...] = jnp.broadcast_to(mixed.astype(BF16)[None], out_ref.shape)


def query_kernel(tok_ref, weight_ref, out_ref):
    project_heads(tok_ref, weight_ref.at[0], head_mean_matrix(), out_ref)


READ_OUT, SELF_Q, SELF_K, SELF_V, SELF_OUT, WRITE_Q, WRITE_K, WRITE_V, WRITE_OUT = range(9)


def write_kernel(
    index_ref,
    scale_ref,
    mix_ref,
    lat_ref,
    weights_ref,
    raw_hbm_ref,
    query_hbm_ref,
    tok_out_ref,
    lat_out_ref,
    weight_ref,
    raw_ref,
    write_q_ref,
    stream_ref,
    normed_ref,
    q_ref,
    k_ref,
    v_ref,
    att_ref,
    write_att_ref,
    sems,
):
    order = (READ_OUT, SELF_Q, SELF_K, SELF_V, SELF_OUT, WRITE_K, WRITE_V, WRITE_OUT)
    copies = {}
    for slot, matrix in enumerate(order):
        copies[matrix] = pltpu.make_async_copy(
            weights_ref.at[matrix], weight_ref.at[slot], sems.at[slot]
        )
    query_copy = pltpu.make_async_copy(query_hbm_ref, write_q_ref, sems.at[len(order)])
    raw_copy = pltpu.make_async_copy(raw_hbm_ref, raw_ref, sems.at[len(order) + 1])
    for matrix in order:
        copies[matrix].start()
    query_copy.start()
    raw_copy.start()

    def ready(matrix):
        copies[matrix].wait()
        return weight_ref.at[order.index(matrix)]

    mean_matrix = head_mean_matrix()
    n_lat = lat_ref.shape[0]
    own_rows = lat_out_ref.shape[0]
    chips, cores, chip_rows, half = mix_ref.shape
    weight = ready(READ_OUT)
    lat_one = lat_ref[...].astype(F32)
    for core in range(cores):
        mix = mix_ref[:, core].reshape(chips * chip_rows, half)
        lat_one += dot(mix, weight[core * half : (core + 1) * half, :])
    stream_ref[...] = lat_one
    normed_ref[...] = norm_rows(lat_one).astype(BF16)
    project_heads(normed_ref, ready(SELF_Q), mean_matrix, q_ref)
    project_heads(normed_ref, ready(SELF_K), mean_matrix, k_ref)
    project_values(normed_ref, ready(SELF_V), v_ref)
    attend_into(q_ref, k_ref, v_ref, scale_ref, 1, att_ref, 6)
    lat_two = stream_ref[...] + dot(att_ref[...], ready(SELF_OUT)[...])
    stream_ref[...] = lat_two
    normed_ref[...] = norm_rows(lat_two).astype(BF16)
    own = pl.ds(pl.multiple_of(index_ref[0] * own_rows, own_rows), own_rows)
    lat_out_ref[...] = stream_ref[own, :]
    project_heads(normed_ref, ready(WRITE_K), mean_matrix, k_ref)
    project_values(normed_ref, ready(WRITE_V), v_ref)
    query_copy.wait()
    attend_into(write_q_ref, k_ref, v_ref, scale_ref, 2, write_att_ref, WRITE_UNROLL)
    weight = ready(WRITE_OUT)
    raw_copy.wait()

    def last(rows):
        update = dot(write_att_ref[rows, :], weight[...])
        tok_out_ref[rows, :] = (raw_ref[rows, :].astype(F32) + update).astype(BF16)

    row_blocks(raw_ref.shape[0], 512, last)


IN_VMEM = pl.BlockSpec(memory_space=pltpu.VMEM)
IN_SMEM = pl.BlockSpec(memory_space=pltpu.SMEM)
IN_PLACE = pl.BlockSpec(memory_space=pl.ANY)


def read_call(core, head_scale, own, peer, blocks, n_lat):
    n_tok, width = own.shape
    half = width // CORES
    devices, n_rows, packed_width = blocks.shape
    return pl.pallas_call(
        read_kernel,
        name="read",
        out_shape=(
            jax.ShapeDtypeStruct((n_lat, half + PAIR), BF16),
            jax.ShapeDtypeStruct((n_lat, width), BF16),
        ),
        in_specs=[IN_SMEM, IN_SMEM] + [IN_PLACE] * 4,
        out_specs=(IN_VMEM, IN_VMEM),
        scratch_shapes=[
            pltpu.VMEM((2 * n_tok, width), BF16),
            pltpu.VMEM((width, 3 * half), BF16),
            pltpu.VMEM((devices, n_rows, packed_width - 3 * half), BF16),
            pltpu.VMEM((n_lat, width), BF16),
            pltpu.VMEM((n_lat, half), BF16),
            pltpu.VMEM((2 * n_tok, half), BF16),
            pltpu.VMEM((2 * n_tok, half), BF16),
            pltpu.VMEM((n_lat, PAIR), F32),
            pltpu.SemaphoreType.DMA((6,)),
        ],
        compiler_params=pltpu.CompilerParams(vmem_limit_bytes=READ_VMEM),
        cost_estimate=pl.CostEstimate(
            flops=20_000_000_000, bytes_accessed=8_000_000, transcendentals=6_300_000
        ),
    )(core, head_scale, own, peer, blocks.reshape(devices * n_rows, packed_width), blocks)


def write_call(index, head_scale, mixed, lat_full, rest, tokens, queries, own_rows):
    n_lat, width = lat_full.shape
    latents_bf16 = pltpu.VMEM((n_lat, width), BF16)
    tokens_bf16 = pltpu.VMEM(tokens.shape, BF16)
    return pl.pallas_call(
        write_kernel,
        name="write",
        out_shape=(
            jax.ShapeDtypeStruct(tokens.shape, BF16),
            jax.ShapeDtypeStruct((own_rows, width), F32),
        ),
        in_specs=[IN_SMEM, IN_SMEM, IN_VMEM, IN_VMEM, IN_PLACE, IN_PLACE, IN_PLACE],
        out_specs=(IN_VMEM, IN_VMEM),
        scratch_shapes=[
            pltpu.VMEM((8, width, width), BF16),
            tokens_bf16,
            tokens_bf16,
            pltpu.VMEM((n_lat, width), F32),
            latents_bf16,
            latents_bf16,
            latents_bf16,
            latents_bf16,
            latents_bf16,
            tokens_bf16,
            pltpu.SemaphoreType.DMA((10,)),
        ],
        compiler_params=pltpu.CompilerParams(vmem_limit_bytes=WRITE_VMEM),
    )(index, head_scale, mixed, lat_full, rest, tokens, queries)


def shards(tokens, latents, read_weights, later_weights, head_scale):
    n_tok, width = tokens.shape
    own_rows = latents.shape[0]
    devices = lax.axis_size("seq")
    chips = devices // CORES
    n_lat = own_rows * devices
    half = width // CORES
    weight_rows = read_weights.shape[1]
    index = lax.axis_index("seq").astype(jnp.int32)
    same_core = [[CORES * chip + core for chip in range(chips)] for core in range(CORES)]
    swap = [(device, device ^ 1) for device in range(devices)]

    packed_width = 3 * half + own_rows * width // weight_rows
    first, rest = pl.pallas_call(
        pack_kernel,
        name="pack",
        out_shape=(
            jax.ShapeDtypeStruct((chips, CORES, weight_rows, packed_width), BF16),
            jax.ShapeDtypeStruct((9, weight_rows, width), BF16),
        ),
        in_specs=[IN_VMEM] * 3,
        out_specs=(IN_VMEM, IN_VMEM),
        compiler_params=pltpu.CompilerParams(vmem_limit_bytes=PACK_VMEM),
    )(read_weights, later_weights, latents)
    first = first.reshape(devices, weight_rows, packed_width)
    first = lax.all_to_all(first, "seq", 0, 0, tiled=True)
    rest = lax.all_gather(rest, "seq", axis=1, tiled=True)
    tok_normed = norm_rows(tokens).astype(BF16)
    peer_normed = lax.ppermute(tok_normed, "seq", swap)
    parts, lat_full = read_call(
        (index % CORES).reshape(1), head_scale, tok_normed, peer_normed, first, n_lat
    )
    queries = pl.pallas_call(
        query_kernel,
        name="query",
        grid=(1,),
        out_shape=jax.ShapeDtypeStruct((n_tok, width), BF16),
        in_specs=[
            pl.BlockSpec((n_tok, width), lambda i: (0, 0)),
            pl.BlockSpec((1, width, width), lambda i: (WRITE_Q, 0, 0)),
        ],
        out_specs=pl.BlockSpec((n_tok, width), lambda i: (0, 0)),
        compiler_params=pltpu.CompilerParams(vmem_limit_bytes=QUERY_VMEM),
        cost_estimate=pl.CostEstimate(
            flops=4_000_000_000, bytes_accessed=5_000_000, transcendentals=800_000
        ),
    )(tok_normed, rest)
    parts = lax.all_to_all(
        parts.reshape(chips, CORES * own_rows, half + PAIR),
        "seq",
        0,
        0,
        tiled=True,
        axis_index_groups=same_core,
    )
    mixed = pl.pallas_call(
        functools.partial(combine_kernel, parts=chips),
        name="combine",
        out_shape=jax.ShapeDtypeStruct((devices, CORES * own_rows, half), BF16),
        in_specs=[IN_VMEM],
        out_specs=IN_VMEM,
        compiler_params=pltpu.CompilerParams(vmem_limit_bytes=COMBINE_VMEM),
    )(parts.reshape(n_lat, half + PAIR))
    mixed = lax.all_to_all(mixed, "seq", 0, 0, tiled=True)
    mixed = mixed.reshape(chips, CORES, CORES * own_rows, half)
    return write_call(
        index.reshape(1), head_scale, mixed, lat_full, rest, tokens, queries, own_rows
    )


def solution(mesh):
    placed = (
        P(("vid", "seq"), None),
        P(("vid", "seq"), None),
        P(None, "seq", None),
        P(None, "seq", None),
        P(),
    )
    return jax.shard_map(
        shards,
        mesh=mesh,
        in_specs=placed,
        out_specs=(P(("vid", "seq"), None), P(("vid", "seq"), None)),
        check_vma=False,
    )
```

```python
import functools
import math

import jax
import jax.numpy as jnp
from jax import lax
from jax.experimental import pallas as pl
from jax.experimental.pallas import tpu as pltpu
from jax.sharding import PartitionSpec as P

HEADS = 12
HEAD_DIM = 64
PAIR = 2 * HEAD_DIM
EPSILON = 1e-06
LOG2E = math.log2(math.e)
BF16 = jnp.bfloat16
F32 = jnp.float32
MIB = 1024 * 1024
PACK_VMEM = 58 * MIB
READ_VMEM = 56 * MIB
COMBINE_VMEM = 40 * MIB
QUERY_VMEM = 50 * MIB
WRITE_VMEM = 50 * MIB
PIECE = 16
TOTALS = 6
CORES = 2
WRITE_UNROLL = 6


def norm_rows(values):
    values = values.astype(F32)
    return values * lax.rsqrt(jnp.mean(values * values, axis=-1, keepdims=True) + EPSILON)


def dot(left, right):
    return jnp.dot(left, right, preferred_element_type=F32)


def dot_nt(left, right):
    return lax.dot_general(left, right, (((1,), (1,)), ((), ())), preferred_element_type=F32)


def head_mean_matrix():
    rows = lax.broadcasted_iota(jnp.int32, (256, 256), 0) // HEAD_DIM
    cols = lax.broadcasted_iota(jnp.int32, (256, 256), 1) // HEAD_DIM
    return jnp.where(rows == cols, 1.0 / HEAD_DIM, 0.0).astype(BF16)


def head_norm(values, mean_matrix):
    squares = values * values
    high = squares.astype(BF16)
    low = (squares - high.astype(F32)).astype(BF16)
    parts = []
    for start in range(0, values.shape[1], 256):
        cols = slice(start, min(start + 256, values.shape[1]))
        size = cols.stop - start
        matrix = mean_matrix[:size, :size]
        mean = dot(high[:, cols], matrix) + dot(low[:, cols], matrix)
        parts.append((values[:, cols] * lax.rsqrt(mean + EPSILON)).astype(BF16))
    return jnp.concatenate(parts, axis=1)


def first_half(shape):
    return lax.broadcasted_iota(jnp.int32, shape, 1) % PAIR < HEAD_DIM


def row_blocks(n_rows, block, body):
    for start in range(0, n_rows, block):
        body(pl.ds(start, block))


def project_heads(x_ref, weight, mean_matrix, out_ref, block=512):
    def body(rows):
        out_ref[rows, :] = head_norm(dot(x_ref[rows, :], weight[...]), mean_matrix)

    row_blocks(x_ref.shape[0], block, body)


def project_values(x_ref, weight, out_ref, block=512):
    def body(rows):
        out_ref[rows, :] = dot(x_ref[rows, :], weight[...]).astype(BF16)

    row_blocks(x_ref.shape[0], block, body)


def attend(q_ref, k_ref, v_ref, factor, emit, block=512, unroll=1):
    n_blocks = q_ref.shape[0] // block
    n_steps = n_blocks * (q_ref.shape[1] // PAIR)

    def step(i, carry):
        pair, row = i // n_blocks, i % n_blocks
        cols, rows = pair * PAIR, row * block
        if not isinstance(i, int):
            cols, rows = pl.multiple_of(cols, PAIR), pl.multiple_of(rows, block)
        cols, rows = pl.ds(cols, PAIR), pl.ds(rows, block)
        queries, keys, values = q_ref[rows, cols], k_ref[:, cols], v_ref[:, cols]
        values = jnp.concatenate([values, jnp.ones_like(values)], axis=1)
        mask = first_half(queries.shape)
        zero = jnp.zeros_like(queries)
        heads = []
        for which in range(2):
            own = (mask, queries, zero) if which == 0 else (mask, zero, queries)
            scores = dot_nt(jnp.where(*own), keys)
            top = jnp.max(scores, axis=1, keepdims=True)
            weights = jnp.exp2((scores - top) * (factor(2 * pair + which) * LOG2E))
            both = dot(weights.astype(BF16), values)
            heads.append((top, both[:, :PAIR], both[:, PAIR:]))
        emit(pair, rows, cols, heads)
        return carry

    if unroll >= n_steps:
        for i in range(n_steps):
            step(i, 0)
    else:
        lax.fori_loop(0, n_steps, step, 0, unroll=unroll)


def attend_into(q_ref, k_ref, v_ref, scale_ref, stage, out_ref, unroll):
    def emit(pair, rows, cols, heads):
        (_, even, even_total), (_, odd, odd_total) = heads
        mask = first_half(even.shape)
        total = jnp.where(mask, even_total, odd_total)
        inverse = pl.reciprocal(total, approx=True)
        inverse = inverse * (2.0 - total * inverse)
        out_ref[rows, cols] = (jnp.where(mask, even, odd) * inverse).astype(BF16)

    def factor(head):
        return scale_ref[stage, head] / math.sqrt(HEAD_DIM)

    attend(q_ref, k_ref, v_ref, factor, emit, unroll=unroll)


def pack_kernel(read_ref, later_ref, lat_ref, first_ref, rest_ref, block_ref, sems):
    _, n_rows, width = read_ref.shape
    own_rows = lat_ref.shape[0]
    half = width // CORES
    n_later = later_ref.shape[0]
    chips = first_ref.shape[0]
    copies = [
        pltpu.make_async_copy(read_ref.at[3], rest_ref.at[0], sems.at[chips]),
        pltpu.make_async_copy(later_ref, rest_ref.at[pl.ds(1, n_later)], sems.at[chips + 1]),
    ]
    for copy in copies:
        copy.start()
    lat = lat_ref[...].astype(F32)
    split = own_rows * width // n_rows
    low = own_rows // 2
    extra = jnp.concatenate([lat[:low, split:], lat[low:, split:]], axis=1)
    extra = jnp.concatenate([lat[:, :split], extra], axis=0).astype(BF16)
    for core in range(CORES):
        cols = slice(core * half, (core + 1) * half)
        block = jnp.concatenate([read_ref[i][:, cols] for i in range(3)] + [extra], axis=1)
        block_ref[core] = block
    for chip in range(chips):
        copies.append(pltpu.make_async_copy(block_ref, first_ref.at[chip], sems.at[chip]))
        copies[-1].start()
    for copy in copies:
        copy.wait()


def unpack_latents(blocks, own_rows, width):
    devices, n_rows, split = blocks.shape
    blocks = blocks.astype(F32)
    low = blocks[:, own_rows:]
    low = jnp.concatenate([low[:, :, : split // 2], low[:, :, split // 2 :]], axis=1)
    high = blocks[:, :own_rows].reshape(devices * own_rows, split)
    return jnp.concatenate([high, low.reshape(devices * own_rows, width - split)], axis=1)


def read_kernel(
    core_ref,
    scale_ref,
    own_hbm_ref,
    peer_hbm_ref,
    first_hbm_ref,
    block_hbm_ref,
    out_ref,
    lat_hbm_ref,
    lat_ref,
    tok_ref,
    weight_ref,
    block_ref,
    normed_ref,
    q_ref,
    k_ref,
    v_ref,
    extra_ref,
    sems,
):
    width = q_ref.shape[1]
    columns = [pl.ds(i * width, width) for i in range(3)]
    block_copy = pltpu.make_async_copy(
        block_hbm_ref.at[:, :, pl.ds(3 * width, block_ref.shape[2])], block_ref, sems.at[0]
    )
    weight_copies = [
        pltpu.make_async_copy(
            first_hbm_ref.at[:, columns[i]], weight_ref.at[:, columns[i]], sems.at[1 + i]
        )
        for i in range(3)
    ]
    n_tok = own_hbm_ref.shape[0]
    own_copy = pltpu.make_async_copy(own_hbm_ref, tok_ref.at[pl.ds(0, n_tok), :], sems.at[4])
    peer_copy = pltpu.make_async_copy(
        peer_hbm_ref, tok_ref.at[pl.ds(n_tok, n_tok), :], sems.at[5]
    )
    for copy in (block_copy, weight_copies[0], own_copy, *weight_copies[1:], peer_copy):
        copy.start()
    mean_matrix = head_mean_matrix()
    n_heads = width // HEAD_DIM
    n_lat, full_width = lat_ref.shape
    block_copy.wait()
    lat = unpack_latents(block_ref[...], n_lat // block_ref.shape[0], full_width)
    lat_ref[...] = lat.astype(BF16)
    lat_copy = pltpu.make_async_copy(lat_ref, lat_hbm_ref, sems.at[6])
    lat_copy.start()
    normed_ref[...] = norm_rows(lat).astype(BF16)
    weight_copies[0].wait()
    project_heads(normed_ref, weight_ref.at[:, columns[0]], mean_matrix, q_ref)
    own_copy.wait()
    for copy in (*weight_copies[1:], peer_copy):
        copy.wait()

    def project_block(i, carry):
        rows = pl.ds(pl.multiple_of(i * 512, 512), 512)
        keys = dot(tok_ref[rows, :], weight_ref[:, columns[1]])
        k_ref[rows, :] = head_norm(keys, mean_matrix)
        v_ref[rows, :] = dot(tok_ref[rows, :], weight_ref[:, columns[2]]).astype(BF16)
        return carry

    lax.fori_loop(0, tok_ref.shape[0] // 512, project_block, 0)
    extra_ref[...] = jnp.zeros_like(extra_ref)

    def factor(head):
        return scale_ref[0, core_ref[0] * n_heads + head] / math.sqrt(HEAD_DIM)

    def emit(pair, rows, cols, heads):
        (_, even, _), (_, odd, _) = heads
        out_ref[rows, cols] = jnp.where(first_half(even.shape), even, odd).astype(BF16)
        lane = lax.broadcasted_iota(jnp.int32, even.shape, 1)
        extra = extra_ref[rows, :]
        for which, (top, _, total) in enumerate(heads):
            head = 2 * pair + which
            extra = jnp.where(lane == head, top * factor(head), extra)
            extra = jnp.where(lane == TOTALS + head, total, extra)
        extra_ref[rows, :] = extra

    attend(q_ref, k_ref, v_ref, factor, emit, unroll=3)
    extra = extra_ref[...]
    high = extra.astype(BF16).astype(F32)
    mid = (extra - high).astype(BF16).astype(F32)
    low = extra - high - mid
    packed = high + pltpu.roll(mid, PIECE, 1) + pltpu.roll(low, 2 * PIECE, 1)
    out_ref[:, width:] = packed.astype(BF16)
    lat_copy.wait()


def combine_kernel(part_ref, out_ref, *, parts):
    width = out_ref.shape[-1]
    rows = out_ref.shape[1]
    lane = lax.broadcasted_iota(jnp.int32, (PAIR, width), 0)
    head = lax.broadcasted_iota(jnp.int32, (PAIR, width), 1) // HEAD_DIM
    pick_top = jnp.zeros((PAIR, width), F32)
    pick_total = jnp.zeros((PAIR, width), F32)
    for piece in range(3):
        pick_top = jnp.where(lane == head + piece * PIECE, 1.0, pick_top)
        pick_total = jnp.where(lane == head + TOTALS + piece * PIECE, 1.0, pick_total)
    extra = part_ref[:, width:]
    shape = (parts, rows, width)
    tops = dot(extra, pick_top.astype(BF16)).reshape(shape)
    totals = dot(extra, pick_total.astype(BF16)).reshape(shape)
    rescale = jnp.exp(tops - jnp.max(tops, axis=0, keepdims=True))
    sums = part_ref[:, :width].astype(F32).reshape(shape)
    mixed = jnp.sum(rescale * sums, axis=0) / jnp.sum(rescale * totals, axis=0)
    out_ref[...] = jnp.broadcast_to(mixed.astype(BF16)[None], out_ref.shape)


def query_kernel(tok_ref, weight_ref, out_ref):
    project_heads(tok_ref, weight_ref.at[0], head_mean_matrix(), out_ref)


READ_OUT, SELF_Q, SELF_K, SELF_V, SELF_OUT, WRITE_Q, WRITE_K, WRITE_V, WRITE_OUT = range(9)


def write_kernel(
    index_ref,
    scale_ref,
    mix_ref,
    lat_ref,
    weights_ref,
    raw_hbm_ref,
    query_hbm_ref,
    tok_out_ref,
    lat_out_ref,
    weight_ref,
    raw_ref,
    write_q_ref,
    stream_ref,
    normed_ref,
    q_ref,
    k_ref,
    v_ref,
    att_ref,
    write_att_ref,
    out_ref,
    sems,
):
    order = (READ_OUT, SELF_Q, SELF_K, SELF_V, SELF_OUT, WRITE_K, WRITE_V, WRITE_OUT)
    copies = {}
    for slot, matrix in enumerate(order):
        copies[matrix] = pltpu.make_async_copy(
            weights_ref.at[matrix], weight_ref.at[slot], sems.at[slot]
        )
    query_copy = pltpu.make_async_copy(query_hbm_ref, write_q_ref, sems.at[len(order)])
    raw_copy = pltpu.make_async_copy(raw_hbm_ref, raw_ref, sems.at[len(order) + 1])
    for matrix in order:
        copies[matrix].start()
    query_copy.start()
    raw_copy.start()

    def ready(matrix):
        copies[matrix].wait()
        return weight_ref.at[order.index(matrix)]

    mean_matrix = head_mean_matrix()
    n_lat = lat_ref.shape[0]
    own_rows = lat_out_ref.shape[0]
    chips, cores, chip_rows, half = mix_ref.shape
    weight = ready(READ_OUT)
    lat_one = lat_ref[...].astype(F32)
    for core in range(cores):
        mix = mix_ref[:, core].reshape(chips * chip_rows, half)
        lat_one += dot(mix, weight[core * half : (core + 1) * half, :])
    stream_ref[...] = lat_one
    normed_ref[...] = norm_rows(lat_one).astype(BF16)
    project_heads(normed_ref, ready(SELF_Q), mean_matrix, q_ref)
    project_heads(normed_ref, ready(SELF_K), mean_matrix, k_ref)
    project_values(normed_ref, ready(SELF_V), v_ref)
    attend_into(q_ref, k_ref, v_ref, scale_ref, 1, att_ref, 6)
    lat_two = stream_ref[...] + dot(att_ref[...], ready(SELF_OUT)[...])
    stream_ref[...] = lat_two
    normed_ref[...] = norm_rows(lat_two).astype(BF16)
    own = pl.ds(pl.multiple_of(index_ref[0] * own_rows, own_rows), own_rows)
    lat_out_ref[...] = stream_ref[own, :]
    project_heads(normed_ref, ready(WRITE_K), mean_matrix, k_ref)
    project_values(normed_ref, ready(WRITE_V), v_ref)
    query_copy.wait()
    attend_into(write_q_ref, k_ref, v_ref, scale_ref, 2, write_att_ref, WRITE_UNROLL)
    weight = ready(WRITE_OUT)
    raw_copy.wait()
    out_copies = []

    def last(rows):
        update = dot(write_att_ref[rows, :], weight[...])
        out_ref[rows, :] = (raw_ref[rows, :].astype(F32) + update).astype(BF16)
        slot = sems.at[len(order) + 2 + len(out_copies)]
        copy = pltpu.make_async_copy(out_ref.at[rows, :], tok_out_ref.at[rows, :], slot)
        copy.start()
        out_copies.append(copy)

    row_blocks(raw_ref.shape[0], 512, last)
    for copy in out_copies:
        copy.wait()


IN_VMEM = pl.BlockSpec(memory_space=pltpu.VMEM)
IN_SMEM = pl.BlockSpec(memory_space=pltpu.SMEM)
IN_PLACE = pl.BlockSpec(memory_space=pl.ANY)


def read_call(core, head_scale, own, peer, blocks, n_lat):
    n_tok, width = own.shape
    half = width // CORES
    devices, n_rows, packed_width = blocks.shape
    return pl.pallas_call(
        read_kernel,
        name="read",
        out_shape=(
            jax.ShapeDtypeStruct((n_lat, half + PAIR), BF16),
            jax.ShapeDtypeStruct((n_lat, width), BF16),
        ),
        in_specs=[IN_SMEM, IN_SMEM] + [IN_PLACE] * 4,
        out_specs=(IN_VMEM, IN_PLACE),
        scratch_shapes=[
            pltpu.VMEM((n_lat, width), BF16),
            pltpu.VMEM((2 * n_tok, width), BF16),
            pltpu.VMEM((width, 3 * half), BF16),
            pltpu.VMEM((devices, n_rows, packed_width - 3 * half), BF16),
            pltpu.VMEM((n_lat, width), BF16),
            pltpu.VMEM((n_lat, half), BF16),
            pltpu.VMEM((2 * n_tok, half), BF16),
            pltpu.VMEM((2 * n_tok, half), BF16),
            pltpu.VMEM((n_lat, PAIR), F32),
            pltpu.SemaphoreType.DMA((7,)),
        ],
        compiler_params=pltpu.CompilerParams(vmem_limit_bytes=READ_VMEM),
        cost_estimate=pl.CostEstimate(
            flops=20_000_000_000, bytes_accessed=8_000_000, transcendentals=6_300_000
        ),
    )(core, head_scale, own, peer, blocks.reshape(devices * n_rows, packed_width), blocks)


def write_call(index, head_scale, mixed, lat_full, rest, tokens, queries, own_rows):
    n_lat, width = lat_full.shape
    latents_bf16 = pltpu.VMEM((n_lat, width), BF16)
    tokens_bf16 = pltpu.VMEM(tokens.shape, BF16)
    return pl.pallas_call(
        write_kernel,
        name="write",
        out_shape=(
            jax.ShapeDtypeStruct(tokens.shape, BF16),
            jax.ShapeDtypeStruct((own_rows, width), F32),
        ),
        in_specs=[IN_SMEM, IN_SMEM, IN_VMEM, IN_VMEM, IN_PLACE, IN_PLACE, IN_PLACE],
        out_specs=(IN_PLACE, IN_VMEM),
        scratch_shapes=[
            pltpu.VMEM((8, width, width), BF16),
            tokens_bf16,
            tokens_bf16,
            pltpu.VMEM((n_lat, width), F32),
            latents_bf16,
            latents_bf16,
            latents_bf16,
            latents_bf16,
            latents_bf16,
            tokens_bf16,
            tokens_bf16,
            pltpu.SemaphoreType.DMA((12,)),
        ],
        compiler_params=pltpu.CompilerParams(vmem_limit_bytes=WRITE_VMEM),
    )(index, head_scale, mixed, lat_full, rest, tokens, queries)


def shards(tokens, latents, read_weights, later_weights, head_scale):
    n_tok, width = tokens.shape
    own_rows = latents.shape[0]
    devices = lax.axis_size("seq")
    chips = devices // CORES
    n_lat = own_rows * devices
    half = width // CORES
    weight_rows = read_weights.shape[1]
    index = lax.axis_index("seq").astype(jnp.int32)
    same_core = [[CORES * chip + core for chip in range(chips)] for core in range(CORES)]
    swap = [(device, device ^ 1) for device in range(devices)]

    packed_width = 3 * half + own_rows * width // weight_rows
    first, rest = pl.pallas_call(
        pack_kernel,
        name="pack",
        out_shape=(
            jax.ShapeDtypeStruct((chips, CORES, weight_rows, packed_width), BF16),
            jax.ShapeDtypeStruct((9, weight_rows, width), BF16),
        ),
        in_specs=[IN_VMEM, IN_PLACE, IN_VMEM],
        out_specs=(IN_PLACE, IN_PLACE),
        scratch_shapes=[
            pltpu.VMEM((CORES, weight_rows, packed_width), BF16),
            pltpu.SemaphoreType.DMA((chips + 2,)),
        ],
        compiler_params=pltpu.CompilerParams(vmem_limit_bytes=PACK_VMEM),
    )(read_weights, later_weights, latents)
    first = first.reshape(devices, weight_rows, packed_width)
    first = lax.all_to_all(first, "seq", 0, 0, tiled=True)
    rest = lax.all_gather(rest, "seq", axis=1, tiled=True)
    tok_normed = norm_rows(tokens).astype(BF16)
    peer_normed = lax.ppermute(tok_normed, "seq", swap)
    parts, lat_full = read_call(
        (index % CORES).reshape(1), head_scale, tok_normed, peer_normed, first, n_lat
    )
    queries = pl.pallas_call(
        query_kernel,
        name="query",
        grid=(1,),
        out_shape=jax.ShapeDtypeStruct((n_tok, width), BF16),
        in_specs=[
            pl.BlockSpec((n_tok, width), lambda i: (0, 0)),
            pl.BlockSpec((1, width, width), lambda i: (WRITE_Q, 0, 0)),
        ],
        out_specs=pl.BlockSpec((n_tok, width), lambda i: (0, 0)),
        compiler_params=pltpu.CompilerParams(vmem_limit_bytes=QUERY_VMEM),
        cost_estimate=pl.CostEstimate(
            flops=4_000_000_000, bytes_accessed=5_000_000, transcendentals=800_000
        ),
    )(tok_normed, rest)
    parts = lax.all_to_all(
        parts.reshape(chips, CORES * own_rows, half + PAIR),
        "seq",
        0,
        0,
        tiled=True,
        axis_index_groups=same_core,
    )
    mixed = pl.pallas_call(
        functools.partial(combine_kernel, parts=chips),
        name="combine",
        out_shape=jax.ShapeDtypeStruct((devices, CORES * own_rows, half), BF16),
        in_specs=[IN_VMEM],
        out_specs=IN_VMEM,
        compiler_params=pltpu.CompilerParams(vmem_limit_bytes=COMBINE_VMEM),
    )(parts.reshape(n_lat, half + PAIR))
    mixed = lax.all_to_all(mixed, "seq", 0, 0, tiled=True)
    mixed = mixed.reshape(chips, CORES, CORES * own_rows, half)
    return write_call(
        index.reshape(1), head_scale, mixed, lat_full, rest, tokens, queries, own_rows
    )


def solution(mesh):
    placed = (
        P(("vid", "seq"), None),
        P(("vid", "seq"), None),
        P(None, "seq", None),
        P(None, "seq", None),
        P(),
    )
    return jax.shard_map(
        shards,
        mesh=mesh,
        in_specs=placed,
        out_specs=(P(("vid", "seq"), None), P(("vid", "seq"), None)),
        check_vma=False,
    )
```

```python
import functools
import math

import jax
import jax.numpy as jnp
from jax import lax
from jax.experimental import pallas as pl
from jax.experimental.pallas import tpu as pltpu
from jax.sharding import PartitionSpec as P

HEADS = 12
HEAD_DIM = 64
PAIR = 2 * HEAD_DIM
EPSILON = 1e-06
LOG2E = math.log2(math.e)
BF16 = jnp.bfloat16
F32 = jnp.float32
MIB = 1024 * 1024
PACK_VMEM = 58 * MIB
READ_VMEM = 56 * MIB
COMBINE_VMEM = 40 * MIB
QUERY_VMEM = 50 * MIB
WRITE_VMEM = 50 * MIB
PIECE = 16
TOTALS = 6
CORES = 2
WRITE_UNROLL = 12


def norm_rows(values):
    values = values.astype(F32)
    return values * lax.rsqrt(jnp.mean(values * values, axis=-1, keepdims=True) + EPSILON)


def dot(left, right):
    return jnp.dot(left, right, preferred_element_type=F32)


def dot_nt(left, right):
    return lax.dot_general(left, right, (((1,), (1,)), ((), ())), preferred_element_type=F32)


def head_mean_matrix():
    rows = lax.broadcasted_iota(jnp.int32, (256, 256), 0) // HEAD_DIM
    cols = lax.broadcasted_iota(jnp.int32, (256, 256), 1) // HEAD_DIM
    return jnp.where(rows == cols, 1.0 / HEAD_DIM, 0.0).astype(BF16)


def head_norm(values, mean_matrix):
    squares = values * values
    high = squares.astype(BF16)
    low = (squares - high.astype(F32)).astype(BF16)
    parts = []
    for start in range(0, values.shape[1], 256):
        cols = slice(start, min(start + 256, values.shape[1]))
        size = cols.stop - start
        matrix = mean_matrix[:size, :size]
        mean = dot(high[:, cols], matrix) + dot(low[:, cols], matrix)
        parts.append((values[:, cols] * lax.rsqrt(mean + EPSILON)).astype(BF16))
    return jnp.concatenate(parts, axis=1)


def first_half(shape):
    return lax.broadcasted_iota(jnp.int32, shape, 1) % PAIR < HEAD_DIM


def row_blocks(n_rows, block, body):
    for start in range(0, n_rows, block):
        body(pl.ds(start, block))


def project_heads(x_ref, weight, mean_matrix, out_ref, block=512):
    def body(rows):
        out_ref[rows, :] = head_norm(dot(x_ref[rows, :], weight[...]), mean_matrix)

    row_blocks(x_ref.shape[0], block, body)


def project_values(x_ref, weight, out_ref, block=512):
    def body(rows):
        out_ref[rows, :] = dot(x_ref[rows, :], weight[...]).astype(BF16)

    row_blocks(x_ref.shape[0], block, body)


def attend(q_ref, k_ref, v_ref, factor, emit, block=512, unroll=1):
    n_blocks = q_ref.shape[0] // block
    n_steps = n_blocks * (q_ref.shape[1] // PAIR)

    def step(i, carry):
        pair, row = i // n_blocks, i % n_blocks
        cols, rows = pair * PAIR, row * block
        if not isinstance(i, int):
            cols, rows = pl.multiple_of(cols, PAIR), pl.multiple_of(rows, block)
        cols, rows = pl.ds(cols, PAIR), pl.ds(rows, block)
        queries, keys, values = q_ref[rows, cols], k_ref[:, cols], v_ref[:, cols]
        values = jnp.concatenate([values, jnp.ones_like(values)], axis=1)
        mask = first_half(queries.shape)
        zero = jnp.zeros_like(queries)
        heads = []
        for which in range(2):
            own = (mask, queries, zero) if which == 0 else (mask, zero, queries)
            scores = dot_nt(jnp.where(*own), keys)
            top = jnp.max(scores, axis=1, keepdims=True)
            weights = jnp.exp2((scores - top) * (factor(2 * pair + which) * LOG2E))
            both = dot(weights.astype(BF16), values)
            heads.append((top, both[:, :PAIR], both[:, PAIR:]))
        emit(pair, rows, cols, heads)
        return carry

    if unroll >= n_steps:
        for i in range(n_steps):
            step(i, 0)
    else:
        lax.fori_loop(0, n_steps, step, 0, unroll=unroll)


def attend_into(q_ref, k_ref, v_ref, scale_ref, stage, out_ref, unroll):
    def emit(pair, rows, cols, heads):
        (_, even, even_total), (_, odd, odd_total) = heads
        mask = first_half(even.shape)
        total = jnp.where(mask, even_total, odd_total)
        inverse = pl.reciprocal(total, approx=True)
        inverse = inverse * (2.0 - total * inverse)
        out_ref[rows, cols] = (jnp.where(mask, even, odd) * inverse).astype(BF16)

    def factor(head):
        return scale_ref[stage, head] / math.sqrt(HEAD_DIM)

    attend(q_ref, k_ref, v_ref, factor, emit, unroll=unroll)


def pack_kernel(read_ref, later_ref, lat_ref, first_ref, rest_ref):
    _, n_rows, width = read_ref.shape
    own_rows = lat_ref.shape[0]
    half = width // CORES
    rest_ref[0] = read_ref[3]
    rest_ref[1:] = later_ref[...]
    lat = lat_ref[...].astype(F32)
    split = own_rows * width // n_rows
    low = own_rows // 2
    extra = jnp.concatenate([lat[:low, split:], lat[low:, split:]], axis=1)
    extra = jnp.concatenate([lat[:, :split], extra], axis=0).astype(BF16)
    for core in range(CORES):
        cols = slice(core * half, (core + 1) * half)
        block = jnp.concatenate([read_ref[i][:, cols] for i in range(3)] + [extra], axis=1)
        first_ref[:, core] = jnp.broadcast_to(block[None], (first_ref.shape[0],) + block.shape)


def unpack_latents(blocks, own_rows, width):
    devices, n_rows, split = blocks.shape
    blocks = blocks.astype(F32)
    low = blocks[:, own_rows:]
    low = jnp.concatenate([low[:, :, : split // 2], low[:, :, split // 2 :]], axis=1)
    high = blocks[:, :own_rows].reshape(devices * own_rows, split)
    return jnp.concatenate([high, low.reshape(devices * own_rows, width - split)], axis=1)


def read_kernel(
    core_ref,
    scale_ref,
    own_hbm_ref,
    peer_hbm_ref,
    first_hbm_ref,
    block_hbm_ref,
    out_ref,
    lat_ref,
    tok_ref,
    weight_ref,
    block_ref,
    normed_ref,
    q_ref,
    k_ref,
    v_ref,
    extra_ref,
    sems,
):
    width = q_ref.shape[1]
    columns = [pl.ds(i * width, width) for i in range(3)]
    block_copy = pltpu.make_async_copy(
        block_hbm_ref.at[:, :, pl.ds(3 * width, block_ref.shape[2])], block_ref, sems.at[0]
    )
    weight_copies = [
        pltpu.make_async_copy(
            first_hbm_ref.at[:, columns[i]], weight_ref.at[:, columns[i]], sems.at[1 + i]
        )
        for i in range(3)
    ]
    n_tok = own_hbm_ref.shape[0]
    own_copy = pltpu.make_async_copy(own_hbm_ref, tok_ref.at[pl.ds(0, n_tok), :], sems.at[4])
    peer_copy = pltpu.make_async_copy(
        peer_hbm_ref, tok_ref.at[pl.ds(n_tok, n_tok), :], sems.at[5]
    )
    for copy in (block_copy, weight_copies[0], own_copy, *weight_copies[1:], peer_copy):
        copy.start()
    mean_matrix = head_mean_matrix()
    n_heads = width // HEAD_DIM
    n_lat, full_width = lat_ref.shape
    block_copy.wait()
    lat = unpack_latents(block_ref[...], n_lat // block_ref.shape[0], full_width)
    lat_ref[...] = lat.astype(BF16)
    normed_ref[...] = norm_rows(lat).astype(BF16)
    weight_copies[0].wait()
    project_heads(normed_ref, weight_ref.at[:, columns[0]], mean_matrix, q_ref)
    own_copy.wait()
    for copy in (*weight_copies[1:], peer_copy):
        copy.wait()

    def project_block(i, carry):
        rows = pl.ds(pl.multiple_of(i * 512, 512), 512)
        keys = dot(tok_ref[rows, :], weight_ref[:, columns[1]])
        k_ref[rows, :] = head_norm(keys, mean_matrix)
        v_ref[rows, :] = dot(tok_ref[rows, :], weight_ref[:, columns[2]]).astype(BF16)
        return carry

    lax.fori_loop(0, tok_ref.shape[0] // 512, project_block, 0)
    extra_ref[...] = jnp.zeros_like(extra_ref)

    def factor(head):
        return scale_ref[0, core_ref[0] * n_heads + head] / math.sqrt(HEAD_DIM)

    def emit(pair, rows, cols, heads):
        (_, even, _), (_, odd, _) = heads
        out_ref[rows, cols] = jnp.where(first_half(even.shape), even, odd).astype(BF16)
        lane = lax.broadcasted_iota(jnp.int32, even.shape, 1)
        extra = extra_ref[rows, :]
        for which, (top, _, total) in enumerate(heads):
            head = 2 * pair + which
            extra = jnp.where(lane == head, top * factor(head), extra)
            extra = jnp.where(lane == TOTALS + head, total, extra)
        extra_ref[rows, :] = extra

    attend(q_ref, k_ref, v_ref, factor, emit, unroll=3)
    extra = extra_ref[...]
    high = extra.astype(BF16).astype(F32)
    mid = (extra - high).astype(BF16).astype(F32)
    low = extra - high - mid
    packed = high + pltpu.roll(mid, PIECE, 1) + pltpu.roll(low, 2 * PIECE, 1)
    out_ref[:, width:] = packed.astype(BF16)


def combine_kernel(part_ref, out_ref, *, parts):
    width = out_ref.shape[-1]
    rows = out_ref.shape[1]
    lane = lax.broadcasted_iota(jnp.int32, (PAIR, width), 0)
    head = lax.broadcasted_iota(jnp.int32, (PAIR, width), 1) // HEAD_DIM
    pick_top = jnp.zeros((PAIR, width), F32)
    pick_total = jnp.zeros((PAIR, width), F32)
    for piece in range(3):
        pick_top = jnp.where(lane == head + piece * PIECE, 1.0, pick_top)
        pick_total = jnp.where(lane == head + TOTALS + piece * PIECE, 1.0, pick_total)
    extra = part_ref[:, width:]
    shape = (parts, rows, width)
    tops = dot(extra, pick_top.astype(BF16)).reshape(shape)
    totals = dot(extra, pick_total.astype(BF16)).reshape(shape)
    rescale = jnp.exp(tops - jnp.max(tops, axis=0, keepdims=True))
    sums = part_ref[:, :width].astype(F32).reshape(shape)
    mixed = jnp.sum(rescale * sums, axis=0) / jnp.sum(rescale * totals, axis=0)
    out_ref[...] = jnp.broadcast_to(mixed.astype(BF16)[None], out_ref.shape)


def query_kernel(tok_ref, weight_ref, out_ref):
    project_heads(tok_ref, weight_ref.at[0], head_mean_matrix(), out_ref)


READ_OUT, SELF_Q, SELF_K, SELF_V, SELF_OUT, WRITE_Q, WRITE_K, WRITE_V, WRITE_OUT = range(9)


def write_kernel(
    index_ref,
    scale_ref,
    mix_ref,
    lat_ref,
    weights_ref,
    raw_hbm_ref,
    query_hbm_ref,
    tok_out_ref,
    lat_out_ref,
    weight_ref,
    raw_ref,
    write_q_ref,
    stream_ref,
    normed_ref,
    q_ref,
    k_ref,
    v_ref,
    att_ref,
    write_att_ref,
    sems,
):
    order = (READ_OUT, SELF_Q, SELF_K, SELF_V, SELF_OUT, WRITE_K, WRITE_V, WRITE_OUT)
    copies = {}
    for slot, matrix in enumerate(order):
        copies[matrix] = pltpu.make_async_copy(
            weights_ref.at[matrix], weight_ref.at[slot], sems.at[slot]
        )
    query_copy = pltpu.make_async_copy(query_hbm_ref, write_q_ref, sems.at[len(order)])
    raw_copy = pltpu.make_async_copy(raw_hbm_ref, raw_ref, sems.at[len(order) + 1])
    for matrix in order:
        copies[matrix].start()
    query_copy.start()
    raw_copy.start()

    def ready(matrix):
        copies[matrix].wait()
        return weight_ref.at[order.index(matrix)]

    mean_matrix = head_mean_matrix()
    n_lat = lat_ref.shape[0]
    own_rows = lat_out_ref.shape[0]
    chips, cores, chip_rows, half = mix_ref.shape
    weight = ready(READ_OUT)
    lat_one = lat_ref[...].astype(F32)
    for core in range(cores):
        mix = mix_ref[:, core].reshape(chips * chip_rows, half)
        lat_one += dot(mix, weight[core * half : (core + 1) * half, :])
    stream_ref[...] = lat_one
    normed_ref[...] = norm_rows(lat_one).astype(BF16)
    project_heads(normed_ref, ready(SELF_Q), mean_matrix, q_ref)
    project_heads(normed_ref, ready(SELF_K), mean_matrix, k_ref)
    project_values(normed_ref, ready(SELF_V), v_ref)
    attend_into(q_ref, k_ref, v_ref, scale_ref, 1, att_ref, 6)
    lat_two = stream_ref[...] + dot(att_ref[...], ready(SELF_OUT)[...])
    stream_ref[...] = lat_two
    normed_ref[...] = norm_rows(lat_two).astype(BF16)
    own = pl.ds(pl.multiple_of(index_ref[0] * own_rows, own_rows), own_rows)
    lat_out_ref[...] = stream_ref[own, :]
    project_heads(normed_ref, ready(WRITE_K), mean_matrix, k_ref)
    project_values(normed_ref, ready(WRITE_V), v_ref)
    query_copy.wait()
    attend_into(write_q_ref, k_ref, v_ref, scale_ref, 2, write_att_ref, WRITE_UNROLL)
    weight = ready(WRITE_OUT)
    raw_copy.wait()

    def last(rows):
        update = dot(write_att_ref[rows, :], weight[...])
        tok_out_ref[rows, :] = (raw_ref[rows, :].astype(F32) + update).astype(BF16)

    row_blocks(raw_ref.shape[0], 512, last)


IN_VMEM = pl.BlockSpec(memory_space=pltpu.VMEM)
IN_SMEM = pl.BlockSpec(memory_space=pltpu.SMEM)
IN_PLACE = pl.BlockSpec(memory_space=pl.ANY)


def read_call(core, head_scale, own, peer, blocks, n_lat):
    n_tok, width = own.shape
    half = width // CORES
    devices, n_rows, packed_width = blocks.shape
    return pl.pallas_call(
        read_kernel,
        name="read",
        out_shape=(
            jax.ShapeDtypeStruct((n_lat, half + PAIR), BF16),
            jax.ShapeDtypeStruct((n_lat, width), BF16),
        ),
        in_specs=[IN_SMEM, IN_SMEM] + [IN_PLACE] * 4,
        out_specs=(IN_VMEM, IN_VMEM),
        scratch_shapes=[
            pltpu.VMEM((2 * n_tok, width), BF16),
            pltpu.VMEM((width, 3 * half), BF16),
            pltpu.VMEM((devices, n_rows, packed_width - 3 * half), BF16),
            pltpu.VMEM((n_lat, width), BF16),
            pltpu.VMEM((n_lat, half), BF16),
            pltpu.VMEM((2 * n_tok, half), BF16),
            pltpu.VMEM((2 * n_tok, half), BF16),
            pltpu.VMEM((n_lat, PAIR), F32),
            pltpu.SemaphoreType.DMA((6,)),
        ],
        compiler_params=pltpu.CompilerParams(vmem_limit_bytes=READ_VMEM),
        cost_estimate=pl.CostEstimate(
            flops=20_000_000_000, bytes_accessed=8_000_000, transcendentals=6_300_000
        ),
    )(core, head_scale, own, peer, blocks.reshape(devices * n_rows, packed_width), blocks)


def write_call(index, head_scale, mixed, lat_full, rest, tokens, queries, own_rows):
    n_lat, width = lat_full.shape
    latents_bf16 = pltpu.VMEM((n_lat, width), BF16)
    tokens_bf16 = pltpu.VMEM(tokens.shape, BF16)
    return pl.pallas_call(
        write_kernel,
        name="write",
        out_shape=(
            jax.ShapeDtypeStruct(tokens.shape, BF16),
            jax.ShapeDtypeStruct((own_rows, width), F32),
        ),
        in_specs=[IN_SMEM, IN_SMEM, IN_VMEM, IN_VMEM, IN_PLACE, IN_PLACE, IN_PLACE],
        out_specs=(IN_VMEM, IN_VMEM),
        scratch_shapes=[
            pltpu.VMEM((8, width, width), BF16),
            tokens_bf16,
            tokens_bf16,
            pltpu.VMEM((n_lat, width), F32),
            latents_bf16,
            latents_bf16,
            latents_bf16,
            latents_bf16,
            latents_bf16,
            tokens_bf16,
            pltpu.SemaphoreType.DMA((10,)),
        ],
        compiler_params=pltpu.CompilerParams(vmem_limit_bytes=WRITE_VMEM),
    )(index, head_scale, mixed, lat_full, rest, tokens, queries)


def shards(tokens, latents, read_weights, later_weights, head_scale):
    n_tok, width = tokens.shape
    own_rows = latents.shape[0]
    devices = lax.axis_size("seq")
    chips = devices // CORES
    n_lat = own_rows * devices
    half = width // CORES
    weight_rows = read_weights.shape[1]
    index = lax.axis_index("seq").astype(jnp.int32)
    same_core = [[CORES * chip + core for chip in range(chips)] for core in range(CORES)]
    swap = [(device, device ^ 1) for device in range(devices)]

    packed_width = 3 * half + own_rows * width // weight_rows
    first, rest = pl.pallas_call(
        pack_kernel,
        name="pack",
        out_shape=(
            jax.ShapeDtypeStruct((chips, CORES, weight_rows, packed_width), BF16),
            jax.ShapeDtypeStruct((9, weight_rows, width), BF16),
        ),
        in_specs=[IN_VMEM] * 3,
        out_specs=(IN_VMEM, IN_VMEM),
        compiler_params=pltpu.CompilerParams(vmem_limit_bytes=PACK_VMEM),
    )(read_weights, later_weights, latents)
    first = first.reshape(devices, weight_rows, packed_width)
    first = lax.all_to_all(first, "seq", 0, 0, tiled=True)
    rest = lax.all_gather(rest, "seq", axis=1, tiled=True)
    tok_normed = norm_rows(tokens).astype(BF16)
    peer_normed = lax.ppermute(tok_normed, "seq", swap)
    parts, lat_full = read_call(
        (index % CORES).reshape(1), head_scale, tok_normed, peer_normed, first, n_lat
    )
    queries = pl.pallas_call(
        query_kernel,
        name="query",
        grid=(1,),
        out_shape=jax.ShapeDtypeStruct((n_tok, width), BF16),
        in_specs=[
            pl.BlockSpec((n_tok, width), lambda i: (0, 0)),
            pl.BlockSpec((1, width, width), lambda i: (WRITE_Q, 0, 0)),
        ],
        out_specs=pl.BlockSpec((n_tok, width), lambda i: (0, 0)),
        compiler_params=pltpu.CompilerParams(vmem_limit_bytes=QUERY_VMEM),
        cost_estimate=pl.CostEstimate(
            flops=4_000_000_000, bytes_accessed=5_000_000, transcendentals=800_000
        ),
    )(tok_normed, rest)
    parts = lax.all_to_all(
        parts.reshape(chips, CORES * own_rows, half + PAIR),
        "seq",
        0,
        0,
        tiled=True,
        axis_index_groups=same_core,
    )
    mixed = pl.pallas_call(
        functools.partial(combine_kernel, parts=chips),
        name="combine",
        out_shape=jax.ShapeDtypeStruct((devices, CORES * own_rows, half), BF16),
        in_specs=[IN_VMEM],
        out_specs=IN_VMEM,
        compiler_params=pltpu.CompilerParams(vmem_limit_bytes=COMBINE_VMEM),
    )(parts.reshape(n_lat, half + PAIR))
    mixed = lax.all_to_all(mixed, "seq", 0, 0, tiled=True)
    mixed = mixed.reshape(chips, CORES, CORES * own_rows, half)
    return write_call(
        index.reshape(1), head_scale, mixed, lat_full, rest, tokens, queries, own_rows
    )


def solution(mesh):
    placed = (
        P(("vid", "seq"), None),
        P(("vid", "seq"), None),
        P(None, "seq", None),
        P(None, "seq", None),
        P(),
    )
    return jax.shard_map(
        shards,
        mesh=mesh,
        in_specs=placed,
        out_specs=(P(("vid", "seq"), None), P(("vid", "seq"), None)),
        check_vma=False,
    )
```

```python
import functools
import math

import jax
import jax.numpy as jnp
from jax import lax
from jax.experimental import pallas as pl
from jax.experimental.pallas import tpu as pltpu
from jax.sharding import PartitionSpec as P

HEADS = 12
HEAD_DIM = 64
PAIR = 2 * HEAD_DIM
EPSILON = 1e-06
LOG2E = math.log2(math.e)
BF16 = jnp.bfloat16
F32 = jnp.float32
MIB = 1024 * 1024
PACK_VMEM = 58 * MIB
READ_VMEM = 40 * MIB
COMBINE_VMEM = 40 * MIB
QUERY_VMEM = 50 * MIB
WRITE_VMEM = 50 * MIB
PIECE = 16
TOTALS = 6
CORES = 2
WRITE_UNROLL = 12


def norm_rows(values):
    values = values.astype(F32)
    return values * lax.rsqrt(jnp.mean(values * values, axis=-1, keepdims=True) + EPSILON)


def dot(left, right):
    return jnp.dot(left, right, preferred_element_type=F32)


def dot_nt(left, right):
    return lax.dot_general(left, right, (((1,), (1,)), ((), ())), preferred_element_type=F32)


def head_mean_matrix():
    rows = lax.broadcasted_iota(jnp.int32, (256, 256), 0) // HEAD_DIM
    cols = lax.broadcasted_iota(jnp.int32, (256, 256), 1) // HEAD_DIM
    return jnp.where(rows == cols, 1.0 / HEAD_DIM, 0.0).astype(BF16)


def head_norm(values, mean_matrix):
    squares = values * values
    high = squares.astype(BF16)
    low = (squares - high.astype(F32)).astype(BF16)
    parts = []
    for start in range(0, values.shape[1], 256):
        cols = slice(start, min(start + 256, values.shape[1]))
        size = cols.stop - start
        matrix = mean_matrix[:size, :size]
        mean = dot(high[:, cols], matrix) + dot(low[:, cols], matrix)
        parts.append((values[:, cols] * lax.rsqrt(mean + EPSILON)).astype(BF16))
    return jnp.concatenate(parts, axis=1)


def first_half(shape):
    return lax.broadcasted_iota(jnp.int32, shape, 1) % PAIR < HEAD_DIM


def row_blocks(n_rows, block, body):
    for start in range(0, n_rows, block):
        body(pl.ds(start, block))


def project_heads(x_ref, weight, mean_matrix, out_ref, block=512):
    def body(rows):
        out_ref[rows, :] = head_norm(dot(x_ref[rows, :], weight[...]), mean_matrix)

    row_blocks(x_ref.shape[0], block, body)


def project_values(x_ref, weight, out_ref, block=512):
    def body(rows):
        out_ref[rows, :] = dot(x_ref[rows, :], weight[...]).astype(BF16)

    row_blocks(x_ref.shape[0], block, body)


def attend(q_ref, k_ref, v_ref, factor, emit, block=512, unroll=1):
    n_blocks = q_ref.shape[0] // block
    n_steps = n_blocks * (q_ref.shape[1] // PAIR)

    def step(i, carry):
        pair, row = i // n_blocks, i % n_blocks
        cols, rows = pair * PAIR, row * block
        if not isinstance(i, int):
            cols, rows = pl.multiple_of(cols, PAIR), pl.multiple_of(rows, block)
        cols, rows = pl.ds(cols, PAIR), pl.ds(rows, block)
        queries, keys, values = q_ref[rows, cols], k_ref[:, cols], v_ref[:, cols]
        values = jnp.concatenate([values, jnp.ones_like(values)], axis=1)
        mask = first_half(queries.shape)
        zero = jnp.zeros_like(queries)
        heads = []
        for which in range(2):
            own = (mask, queries, zero) if which == 0 else (mask, zero, queries)
            scores = dot_nt(jnp.where(*own), keys)
            top = jnp.max(scores, axis=1, keepdims=True)
            weights = jnp.exp2((scores - top) * (factor(2 * pair + which) * LOG2E))
            both = dot(weights.astype(BF16), values)
            heads.append((top, both[:, :PAIR], both[:, PAIR:]))
        emit(pair, rows, cols, heads)
        return carry

    if unroll >= n_steps:
        for i in range(n_steps):
            step(i, 0)
    else:
        lax.fori_loop(0, n_steps, step, 0, unroll=unroll)


def attend_into(q_ref, k_ref, v_ref, scale_ref, stage, out_ref, unroll):
    def emit(pair, rows, cols, heads):
        (_, even, even_total), (_, odd, odd_total) = heads
        mask = first_half(even.shape)
        total = jnp.where(mask, even_total, odd_total)
        inverse = pl.reciprocal(total, approx=True)
        inverse = inverse * (2.0 - total * inverse)
        out_ref[rows, cols] = (jnp.where(mask, even, odd) * inverse).astype(BF16)

    def factor(head):
        return scale_ref[stage, head] / math.sqrt(HEAD_DIM)

    attend(q_ref, k_ref, v_ref, factor, emit, unroll=unroll)


def pack_kernel(read_ref, later_ref, lat_ref, first_ref, rest_ref):
    _, n_rows, width = read_ref.shape
    own_rows = lat_ref.shape[0]
    half = width // CORES
    rest_ref[0] = read_ref[3]
    rest_ref[1:] = later_ref[...]
    lat = lat_ref[...].astype(F32)
    split = own_rows * width // n_rows
    low = own_rows // 2
    extra = jnp.concatenate([lat[:low, split:], lat[low:, split:]], axis=1)
    extra = jnp.concatenate([lat[:, :split], extra], axis=0).astype(BF16)
    for core in range(CORES):
        cols = slice(core * half, (core + 1) * half)
        block = jnp.concatenate([read_ref[i][:, cols] for i in range(3)] + [extra], axis=1)
        first_ref[:, core] = jnp.broadcast_to(block[None], (first_ref.shape[0],) + block.shape)


def unpack_latents(blocks, own_rows, width):
    devices, n_rows, split = blocks.shape
    blocks = blocks.astype(F32)
    low = blocks[:, own_rows:]
    low = jnp.concatenate([low[:, :, : split // 2], low[:, :, split // 2 :]], axis=1)
    high = blocks[:, :own_rows].reshape(devices * own_rows, split)
    return jnp.concatenate([high, low.reshape(devices * own_rows, width - split)], axis=1)


def read_kernel(
    core_ref,
    scale_ref,
    own_hbm_ref,
    peer_hbm_ref,
    first_hbm_ref,
    block_hbm_ref,
    out_ref,
    lat_hbm_ref,
    lat_ref,
    tok_ref,
    weight_ref,
    block_ref,
    normed_ref,
    q_ref,
    k_ref,
    v_ref,
    extra_ref,
    sems,
):
    width = q_ref.shape[1]
    columns = [pl.ds(i * width, width) for i in range(3)]
    block_copy = pltpu.make_async_copy(
        block_hbm_ref.at[:, :, pl.ds(3 * width, block_ref.shape[2])], block_ref, sems.at[0]
    )
    weight_copies = [
        pltpu.make_async_copy(
            first_hbm_ref.at[:, columns[i]], weight_ref.at[:, columns[i]], sems.at[1 + i]
        )
        for i in range(3)
    ]
    n_tok = own_hbm_ref.shape[0]
    own_copy = pltpu.make_async_copy(own_hbm_ref, tok_ref.at[pl.ds(0, n_tok), :], sems.at[4])
    peer_copy = pltpu.make_async_copy(
        peer_hbm_ref, tok_ref.at[pl.ds(n_tok, n_tok), :], sems.at[5]
    )
    for copy in (block_copy, weight_copies[0], own_copy, *weight_copies[1:], peer_copy):
        copy.start()
    mean_matrix = head_mean_matrix()
    n_heads = width // HEAD_DIM
    n_lat, full_width = lat_ref.shape
    block_copy.wait()
    lat = unpack_latents(block_ref[...], n_lat // block_ref.shape[0], full_width)
    lat_ref[...] = lat.astype(BF16)
    lat_copy = pltpu.make_async_copy(lat_ref, lat_hbm_ref, sems.at[6])
    lat_copy.start()
    normed_ref[...] = norm_rows(lat).astype(BF16)
    weight_copies[0].wait()
    project_heads(normed_ref, weight_ref.at[:, columns[0]], mean_matrix, q_ref)
    own_copy.wait()
    for copy in (*weight_copies[1:], peer_copy):
        copy.wait()

    def project_block(i, carry):
        rows = pl.ds(pl.multiple_of(i * 512, 512), 512)
        keys = dot(tok_ref[rows, :], weight_ref[:, columns[1]])
        k_ref[rows, :] = head_norm(keys, mean_matrix)
        v_ref[rows, :] = dot(tok_ref[rows, :], weight_ref[:, columns[2]]).astype(BF16)
        return carry

    lax.fori_loop(0, tok_ref.shape[0] // 512, project_block, 0)
    extra_ref[...] = jnp.zeros_like(extra_ref)

    def factor(head):
        return scale_ref[0, core_ref[0] * n_heads + head] / math.sqrt(HEAD_DIM)

    def emit(pair, rows, cols, heads):
        (_, even, _), (_, odd, _) = heads
        out_ref[rows, cols] = jnp.where(first_half(even.shape), even, odd).astype(BF16)
        lane = lax.broadcasted_iota(jnp.int32, even.shape, 1)
        extra = extra_ref[rows, :]
        for which, (top, _, total) in enumerate(heads):
            head = 2 * pair + which
            extra = jnp.where(lane == head, top * factor(head), extra)
            extra = jnp.where(lane == TOTALS + head, total, extra)
        extra_ref[rows, :] = extra

    attend(q_ref, k_ref, v_ref, factor, emit, unroll=3)
    extra = extra_ref[...]
    high = extra.astype(BF16).astype(F32)
    mid = (extra - high).astype(BF16).astype(F32)
    low = extra - high - mid
    packed = high + pltpu.roll(mid, PIECE, 1) + pltpu.roll(low, 2 * PIECE, 1)
    out_ref[:, width:] = packed.astype(BF16)
    lat_copy.wait()


def combine_kernel(part_ref, out_ref, *, parts):
    width = out_ref.shape[-1]
    rows = out_ref.shape[1]
    lane = lax.broadcasted_iota(jnp.int32, (PAIR, width), 0)
    head = lax.broadcasted_iota(jnp.int32, (PAIR, width), 1) // HEAD_DIM
    pick_top = jnp.zeros((PAIR, width), F32)
    pick_total = jnp.zeros((PAIR, width), F32)
    for piece in range(3):
        pick_top = jnp.where(lane == head + piece * PIECE, 1.0, pick_top)
        pick_total = jnp.where(lane == head + TOTALS + piece * PIECE, 1.0, pick_total)
    extra = part_ref[:, width:]
    shape = (parts, rows, width)
    tops = dot(extra, pick_top.astype(BF16)).reshape(shape)
    totals = dot(extra, pick_total.astype(BF16)).reshape(shape)
    rescale = jnp.exp(tops - jnp.max(tops, axis=0, keepdims=True))
    sums = part_ref[:, :width].astype(F32).reshape(shape)
    mixed = jnp.sum(rescale * sums, axis=0) / jnp.sum(rescale * totals, axis=0)
    out_ref[...] = jnp.broadcast_to(mixed.astype(BF16)[None], out_ref.shape)


def query_kernel(tok_ref, weight_ref, out_ref):
    project_heads(tok_ref, weight_ref.at[0], head_mean_matrix(), out_ref)


READ_OUT, SELF_Q, SELF_K, SELF_V, SELF_OUT, WRITE_Q, WRITE_K, WRITE_V, WRITE_OUT = range(9)


def write_kernel(
    index_ref,
    scale_ref,
    mix_ref,
    lat_ref,
    weights_ref,
    raw_hbm_ref,
    query_hbm_ref,
    tok_out_ref,
    lat_out_ref,
    weight_ref,
    raw_ref,
    write_q_ref,
    stream_ref,
    normed_ref,
    q_ref,
    k_ref,
    v_ref,
    att_ref,
    write_att_ref,
    sems,
):
    order = (READ_OUT, SELF_Q, SELF_K, SELF_V, SELF_OUT, WRITE_K, WRITE_V, WRITE_OUT)
    copies = {}
    for slot, matrix in enumerate(order):
        copies[matrix] = pltpu.make_async_copy(
            weights_ref.at[matrix], weight_ref.at[slot], sems.at[slot]
        )
    query_copy = pltpu.make_async_copy(query_hbm_ref, write_q_ref, sems.at[len(order)])
    raw_copy = pltpu.make_async_copy(raw_hbm_ref, raw_ref, sems.at[len(order) + 1])
    for matrix in order:
        copies[matrix].start()
    query_copy.start()
    raw_copy.start()

    def ready(matrix):
        copies[matrix].wait()
        return weight_ref.at[order.index(matrix)]

    mean_matrix = head_mean_matrix()
    n_lat = lat_ref.shape[0]
    own_rows = lat_out_ref.shape[0]
    chips, cores, chip_rows, half = mix_ref.shape
    weight = ready(READ_OUT)
    lat_one = lat_ref[...].astype(F32)
    for core in range(cores):
        mix = mix_ref[:, core].reshape(chips * chip_rows, half)
        lat_one += dot(mix, weight[core * half : (core + 1) * half, :])
    stream_ref[...] = lat_one
    normed_ref[...] = norm_rows(lat_one).astype(BF16)
    project_heads(normed_ref, ready(SELF_Q), mean_matrix, q_ref)
    project_heads(normed_ref, ready(SELF_K), mean_matrix, k_ref)
    project_values(normed_ref, ready(SELF_V), v_ref)
    attend_into(q_ref, k_ref, v_ref, scale_ref, 1, att_ref, 6)
    lat_two = stream_ref[...] + dot(att_ref[...], ready(SELF_OUT)[...])
    stream_ref[...] = lat_two
    normed_ref[...] = norm_rows(lat_two).astype(BF16)
    own = pl.ds(pl.multiple_of(index_ref[0] * own_rows, own_rows), own_rows)
    lat_out_ref[...] = stream_ref[own, :]
    project_heads(normed_ref, ready(WRITE_K), mean_matrix, k_ref)
    project_values(normed_ref, ready(WRITE_V), v_ref)
    query_copy.wait()
    attend_into(write_q_ref, k_ref, v_ref, scale_ref, 2, write_att_ref, WRITE_UNROLL)
    weight = ready(WRITE_OUT)
    raw_copy.wait()

    def last(rows):
        update = dot(write_att_ref[rows, :], weight[...])
        tok_out_ref[rows, :] = (raw_ref[rows, :].astype(F32) + update).astype(BF16)

    row_blocks(raw_ref.shape[0], 512, last)


IN_VMEM = pl.BlockSpec(memory_space=pltpu.VMEM)
IN_SMEM = pl.BlockSpec(memory_space=pltpu.SMEM)
IN_PLACE = pl.BlockSpec(memory_space=pl.ANY)


def read_call(core, head_scale, own, peer, blocks, n_lat):
    n_tok, width = own.shape
    half = width // CORES
    devices, n_rows, packed_width = blocks.shape
    return pl.pallas_call(
        read_kernel,
        name="read",
        out_shape=(
            jax.ShapeDtypeStruct((n_lat, half + PAIR), BF16),
            jax.ShapeDtypeStruct((n_lat, width), BF16),
        ),
        in_specs=[IN_SMEM, IN_SMEM] + [IN_PLACE] * 4,
        out_specs=(IN_VMEM, pl.BlockSpec(memory_space=pltpu.HBM)),
        scratch_shapes=[
            pltpu.VMEM((n_lat, width), BF16),
            pltpu.VMEM((2 * n_tok, width), BF16),
            pltpu.VMEM((width, 3 * half), BF16),
            pltpu.VMEM((devices, n_rows, packed_width - 3 * half), BF16),
            pltpu.VMEM((n_lat, width), BF16),
            pltpu.VMEM((n_lat, half), BF16),
            pltpu.VMEM((2 * n_tok, half), BF16),
            pltpu.VMEM((2 * n_tok, half), BF16),
            pltpu.VMEM((n_lat, PAIR), F32),
            pltpu.SemaphoreType.DMA((7,)),
        ],
        compiler_params=pltpu.CompilerParams(vmem_limit_bytes=READ_VMEM),
        cost_estimate=pl.CostEstimate(
            flops=20_000_000_000, bytes_accessed=8_000_000, transcendentals=6_300_000
        ),
    )(core, head_scale, own, peer, blocks.reshape(devices * n_rows, packed_width), blocks)


def write_call(index, head_scale, mixed, lat_full, rest, tokens, queries, own_rows):
    n_lat, width = lat_full.shape
    latents_bf16 = pltpu.VMEM((n_lat, width), BF16)
    tokens_bf16 = pltpu.VMEM(tokens.shape, BF16)
    return pl.pallas_call(
        write_kernel,
        name="write",
        out_shape=(
            jax.ShapeDtypeStruct(tokens.shape, BF16),
            jax.ShapeDtypeStruct((own_rows, width), F32),
        ),
        in_specs=[IN_SMEM, IN_SMEM, IN_VMEM, IN_VMEM, IN_PLACE, IN_PLACE, IN_PLACE],
        out_specs=(IN_VMEM, IN_VMEM),
        scratch_shapes=[
            pltpu.VMEM((8, width, width), BF16),
            tokens_bf16,
            tokens_bf16,
            pltpu.VMEM((n_lat, width), F32),
            latents_bf16,
            latents_bf16,
            latents_bf16,
            latents_bf16,
            latents_bf16,
            tokens_bf16,
            pltpu.SemaphoreType.DMA((10,)),
        ],
        compiler_params=pltpu.CompilerParams(vmem_limit_bytes=WRITE_VMEM),
    )(index, head_scale, mixed, lat_full, rest, tokens, queries)


def shards(tokens, latents, read_weights, later_weights, head_scale):
    n_tok, width = tokens.shape
    own_rows = latents.shape[0]
    devices = lax.axis_size("seq")
    chips = devices // CORES
    n_lat = own_rows * devices
    half = width // CORES
    weight_rows = read_weights.shape[1]
    index = lax.axis_index("seq").astype(jnp.int32)
    same_core = [[CORES * chip + core for chip in range(chips)] for core in range(CORES)]
    swap = [(device, device ^ 1) for device in range(devices)]

    packed_width = 3 * half + own_rows * width // weight_rows
    first, rest = pl.pallas_call(
        pack_kernel,
        name="pack",
        out_shape=(
            jax.ShapeDtypeStruct((chips, CORES, weight_rows, packed_width), BF16),
            jax.ShapeDtypeStruct((9, weight_rows, width), BF16),
        ),
        in_specs=[IN_VMEM] * 3,
        out_specs=(IN_VMEM, IN_VMEM),
        compiler_params=pltpu.CompilerParams(vmem_limit_bytes=PACK_VMEM),
    )(read_weights, later_weights, latents)
    first = first.reshape(devices, weight_rows, packed_width)
    first = lax.all_to_all(first, "seq", 0, 0, tiled=True)
    rest = lax.all_gather(rest, "seq", axis=1, tiled=True)
    tok_normed = norm_rows(tokens).astype(BF16)
    peer_normed = lax.ppermute(tok_normed, "seq", swap)
    parts, lat_full = read_call(
        (index % CORES).reshape(1), head_scale, tok_normed, peer_normed, first, n_lat
    )
    queries = pl.pallas_call(
        query_kernel,
        name="query",
        grid=(1,),
        out_shape=jax.ShapeDtypeStruct((n_tok, width), BF16),
        in_specs=[
            pl.BlockSpec((n_tok, width), lambda i: (0, 0)),
            pl.BlockSpec((1, width, width), lambda i: (WRITE_Q, 0, 0)),
        ],
        out_specs=pl.BlockSpec((n_tok, width), lambda i: (0, 0)),
        compiler_params=pltpu.CompilerParams(vmem_limit_bytes=QUERY_VMEM),
        cost_estimate=pl.CostEstimate(
            flops=4_000_000_000, bytes_accessed=5_000_000, transcendentals=800_000
        ),
    )(tok_normed, rest)
    parts = lax.all_to_all(
        parts.reshape(chips, CORES * own_rows, half + PAIR),
        "seq",
        0,
        0,
        tiled=True,
        axis_index_groups=same_core,
    )
    mixed = pl.pallas_call(
        functools.partial(combine_kernel, parts=chips),
        name="combine",
        out_shape=jax.ShapeDtypeStruct((devices, CORES * own_rows, half), BF16),
        in_specs=[IN_VMEM],
        out_specs=IN_VMEM,
        compiler_params=pltpu.CompilerParams(vmem_limit_bytes=COMBINE_VMEM),
    )(parts.reshape(n_lat, half + PAIR))
    mixed = lax.all_to_all(mixed, "seq", 0, 0, tiled=True)
    mixed = mixed.reshape(chips, CORES, CORES * own_rows, half)
    return write_call(
        index.reshape(1), head_scale, mixed, lat_full, rest, tokens, queries, own_rows
    )


def solution(mesh):
    placed = (
        P(("vid", "seq"), None),
        P(("vid", "seq"), None),
        P(None, "seq", None),
        P(None, "seq", None),
        P(),
    )
    return jax.shard_map(
        shards,
        mesh=mesh,
        in_specs=placed,
        out_specs=(P(("vid", "seq"), None), P(("vid", "seq"), None)),
        check_vma=False,
    )
```
